256 devices in a mesh: freq: 4 (over z_hi), rows: 64 (over y, z_lo, x, core).
Axes of the slice: x: 4, y: 4, z: 8 (z_hi: 4, z_lo: 2; z = z_hi * 2 + z_lo), core: 2. Of those that a mesh axis runs over, the one named last changes fastest.
Arguments:
- reflection: bfloat16 [32, 2, 2048, 2048], P('freq', None, 'rows'), may hold values from -0.25 to 0.25
- focus_direct: bfloat16 [32, 2048, 128], P('freq', 'rows'), may hold values from -6 to 6
- onsets: int32 [2048, 64], P('rows'), may hold values from 8 to 63
Outputs:
- focus_plus: bfloat16 [32, 2048, 128], P('freq', 'rows')
- focus_minus: bfloat16 [32, 2048, 128], P('freq', 'rows')
The draws below stay inside these ranges and needn't reach their ends.
All inputs are finite; a program needn't handle non-finite values.
Results may differ from the reference program's by a relative error of at most 0.015.
Values may be sent and summed in bfloat16 or wider, within the bound.
A program may use at most 128 MiB of HBM per device.

```python
import math
import jax
import jax.numpy as jnp
from jax import lax

NP = 64
NT = 128
ITERS = 2
NF = 32
NR = 2048


def touch_ends(array, rng, low, top_value):
    extent = array.shape
    spot = [jax.random.randint(jax.random.fold_in(rng, axis), (), 0, extent[axis]) for axis in range(len(extent))]
    array = array.at[tuple(spot)].set(low)
    longest = extent.index(max(extent))
    spot[longest] = (spot[longest] + 1) % extent[longest]
    return array.at[tuple(spot)].set(top_value)


def with_spikes(values, key, source, target, blocks, factor):
    def block_of(axis_at):
        return (jnp.arange(values.shape[axis_at]) // (values.shape[axis_at] // blocks)).reshape((-1,) + (1,) * (values.ndim - 1 - axis_at))

    near = jax.random.permutation(key, blocks)[block_of(target)]
    other_side = (block_of(target) + blocks // 2) % blocks
    return jnp.where((block_of(source) == near) | (block_of(source) == other_side), factor * values, values)


def steps_of(stream_key, dims, cuts, least, high):
    factor_of, own = 1.0, jax.random.fold_in(stream_key, 6)
    for dim, shards_of in cuts:
        draws = jnp.exp(jax.random.uniform(jax.random.fold_in(own, dim), (shards_of,), jnp.float32, least / len(cuts), high / len(cuts)))
        factor_of = factor_of * jnp.repeat(draws, dims[dim] // shards_of).reshape([-1 if axis == dim else 1 for axis in range(len(dims))])
    return factor_of


def gaussian(own_key, extent, spread, most, cuts=(), held_as=jnp.bfloat16):
    level = steps_of(own_key, extent, cuts, -0.22, 0.18) if cuts else 1.0
    values = jax.random.normal(own_key, extent, jnp.float32) * spread * level
    return jnp.minimum(jnp.maximum(values, -most), most).astype(held_as)


def gaussian_with(key, dims, spread, reach, pieces, heavy, held_as=jnp.bfloat16):
    drawn = spread * jax.random.normal(key, dims, jnp.float32)
    if pieces:
        drawn = drawn * steps_of(key, dims, pieces, -0.22, 0.18)
    return jnp.clip(with_spikes(drawn, jax.random.fold_in(key, 3), *heavy), -reach, reach).astype(held_as)


def setup_inputs(seed: int = 0) -> dict:
    streams_of = jax.random.split(jax.random.key(seed), 4)
    return {
        "reflection": gaussian_with(streams_of[0], (NF, 2, NR, NR), (2 * NR) ** -0.5, 0.25, ((0, 4), (2, 64)), (2, 3, 64, 4.0)),
        "focus_direct": gaussian(streams_of[1], (NF, NR, 2 * NP), 1.0, 6.0, ((0, 4), (1, 64))),
        "onsets": touch_ends(jax.random.randint(streams_of[2], (NR, NP), NT // 16, NT // 2), jax.random.fold_in(streams_of[2], 1), NT // 16, (NT // 2) - 1).astype(jnp.int32),
    }


def spectra_tables(freq_total, temporal_ticks):
    spectral_axis_values = jnp.arange(1, freq_total + 1, dtype=jnp.int32)
    temporal_moments = jnp.arange(temporal_ticks, dtype=jnp.int32)
    rotation_angles_matrix = (temporal_moments[:, None] * spectral_axis_values[None, :]) % temporal_ticks
    angles = rotation_angles_matrix.astype(jnp.float32) * jnp.float32(2.0 * math.pi / temporal_ticks)
    return jnp.cos(angles), jnp.sin(angles)


def mask_table(gate_starting_tiles, temporal_ticks):
    temporal_moments = jnp.arange(temporal_ticks, dtype=jnp.int32)[:, None, None]
    inside_gate_mask = (temporal_moments < gate_starting_tiles[None]) | ((temporal_ticks - temporal_moments) < gate_starting_tiles[None])
    return inside_gate_mask.astype(jnp.float32)


def window_spectra(fourier_coefficients, mask, cosinus_factor, sine):
    temporal_ticks = cosinus_factor.shape[0]
    half_cols = fourier_coefficients.shape[-1] // 2
    values = fourier_coefficients.astype(jnp.float32)
    real_part = values[..., :half_cols]
    imag_part = values[..., half_cols:]
    highest_mode = lax.Precision.HIGHEST
    traces = 2.0 * (jnp.einsum("tk,krp->trp", cosinus_factor, real_part, precision=highest_mode)
                    - jnp.einsum("tk,krp->trp", sine, imag_part, precision=highest_mode))
    kept_traces = traces * mask
    new_real = jnp.einsum("tk,trp->krp", cosinus_factor, kept_traces, precision=highest_mode) / temporal_ticks
    new_imag = -jnp.einsum("tk,trp->krp", sine, kept_traces, precision=highest_mode) / temporal_ticks
    return jnp.concatenate([new_real, new_imag], axis=-1)


def forward_combine(with_real, with_imag, half_cols):
    real_out = with_real[..., :half_cols] - with_imag[..., half_cols:]
    imag_out = with_real[..., half_cols:] + with_imag[..., :half_cols]
    return jnp.concatenate([real_out, imag_out], axis=-1)


def adjoint_combine(with_real, with_imag, half_cols):
    real_out = with_real[..., :half_cols] + with_imag[..., half_cols:]
    imag_out = with_real[..., half_cols:] - with_imag[..., :half_cols]
    return jnp.concatenate([real_out, imag_out], axis=-1)


def reference(reflection, focus_direct, onsets):
    cosinus_factor, sine = spectra_tables(NF, NT)
    mask = mask_table(onsets, NT)
    half_cols = focus_direct.shape[-1] // 2
    wide_reflection = reflection.astype(jnp.float32)
    broad_direct_arrival = focus_direct.astype(jnp.float32)
    plus = focus_direct
    minus = focus_direct
    for step in range(ITERS):
        phase_product = jnp.einsum("fcrs,fsq->fcrq", wide_reflection, plus.astype(jnp.float32))
        convolved = forward_combine(phase_product[:, 0], phase_product[:, 1], half_cols).astype(jnp.bfloat16)
        minus = window_spectra(convolved, mask, cosinus_factor, sine).astype(jnp.bfloat16)
        terms = jnp.einsum("fcrs,frq->fcsq", wide_reflection, minus.astype(jnp.float32))
        correlated = adjoint_combine(terms[:, 0], terms[:, 1], half_cols)
        plus = (broad_direct_arrival + window_spectra(correlated, mask, cosinus_factor, sine)).astype(jnp.bfloat16)
    return plus, minus
```

```python
import math

import jax
import jax.numpy as jnp
import numpy as np
from jax import lax
from jax.experimental import pallas as pl
from jax.experimental.pallas import tpu as pltpu
from jax.sharding import PartitionSpec as P

NT = 128
ITERS = 2
MESH = pl.DeviceIdType.MESH
BF = jnp.bfloat16
F32 = jnp.float32


def window_tables():
    t = np.arange(64)[:, None]
    k = np.arange(1, 33)[None, :]
    ang = 2.0 * np.pi * ((t * k) % NT) / NT
    parts = np.stack([np.cos(ang), np.sin(ang)])
    eye = np.eye(8)
    first = np.einsum("ctf,rs->trcfs", parts, eye).reshape(512, 512)
    weight = np.where(np.arange(64) == 0, 2.0, 4.0) / NT
    back = parts * weight[None, :, None]
    second = np.einsum("ctgf,rs->gcfrts", back.reshape(2, 64, 4, 8), eye).reshape(4, 128, 512)
    return first.astype(jnp.bfloat16), second.astype(jnp.bfloat16)


def turned(block, sign):
    real, imag = block[:, :64], block[:, 64:]
    if sign > 0:
        return jnp.concatenate([-imag, real], axis=1)
    return jnp.concatenate([imag, -real], axis=1)


def kernel(refl, direct, onsets, first, second, plus_out, minus_out,
           rsend, rblk, rtrans, plus, pblk, s1, r1, xf1, minus, mblk, s2, r2, xf2, onw,
           rsnd, rrcv, ssem, rsem):
    fme = lax.axis_index("freq")
    row = lax.axis_index("rows")
    c = lax.rem(row, 2)
    x = lax.rem(row // 2, 4)
    z = lax.rem(row // 8, 2)
    y = row // 16
    zero = c == 0
    u = jnp.where(zero, y, x)
    v = jnp.where(zero, x, y)

    def rows(y, z, x, c):
        return ((y * 2 + z) * 4 + x) * 2 + c

    def wrap(a):
        return lax.rem(a + 8, 4)

    def ring_u(du, dz):
        up, zp = wrap(u + du), lax.rem(z + dz, 2)
        return (fme, jnp.where(zero, rows(up, zp, x, c), rows(y, zp, up, c)))

    def to_ring(d, cp):
        return (fme, rows(y, z, wrap(x + d), 0) if cp == 0 else rows(wrap(y + d), z, x, 1))

    def on_ring(d, cp):
        vp = wrap(v + d)
        return (fme, jnp.where(zero, rows(y, z, vp, cp), rows(vp, z, x, cp)))

    partner = (fme, rows(y, z, x, 1 - c))

    def freq_on(d):
        return (wrap(fme + d), row)

    bar = pltpu.get_barrier_semaphore()
    peers = [partner]
    peers += [ring_u(du, dz) for du in range(4) for dz in range(2) if (du, dz) != (0, 0)]
    peers += [to_ring(d, cp) for d in range(1, 4) for cp in range(2)]
    peers += [on_ring(d, cp) for d in range(1, 4) for cp in range(2)]
    peers += [freq_on(d) for d in range(1, 4)]
    for q in peers:
        pl.semaphore_signal(bar, inc=1, device_id=q, device_id_type=MESH)

    def copy(src, dst, send, recv, device):
        return pltpu.make_async_remote_copy(
            src_ref=src, dst_ref=dst, send_sem=send, recv_sem=recv, device_id=device, device_id_type=MESH)

    def pieces(cp, w):
        if cp == 0:
            return [(k * 256 + w * 64) for k in range(8)]
        return [((w * 2 + k % 2) * 256 + (k // 2) * 64 + 32) for k in range(8)]

    def arrange(cp):
        def step(f, carry):
            block = refl[f].reshape(64, 2048)
            for w in range(4):
                out = jnp.concatenate([block[:, p:p + 32] for p in pieces(cp, w)], axis=1)
                rsend[cp * 4 + w, f] = out.reshape(2, 32, 256)
            return carry
        lax.fori_loop(0, 8, step, 0)

    mine = v * 2 + c

    def send_reflection(d, cp):
        w = wrap((x if cp == 0 else y) + d)
        slot = (x if cp == 0 else y) * 2 + c
        return copy(rsend.at[cp * 4 + w], rblk.at[:, :, pl.ds(pl.multiple_of(slot * 32, 32), 32), :],
                    rsnd.at[d * 2 + cp], rrcv.at[d * 2 + c], to_ring(d, cp))

    def partner_reflection():
        other = 1 - c
        w = jnp.where(zero, y, x)
        slot = jnp.where(zero, y, x) * 2 + c
        return copy(rsend.at[other * 4 + w], rblk.at[:, :, pl.ds(pl.multiple_of(slot * 32, 32), 32), :],
                    rsnd.at[0], rrcv.at[c], partner)

    def recv_reflection(d, cs):
        slot = wrap(v - d) * 2 + cs
        return copy(rsend.at[0], rblk.at[:, :, pl.ds(pl.multiple_of(slot * 32, 32), 32), :],
                    rsnd.at[0], rrcv.at[d * 2 + cs], partner)

    arrange(0)
    plus[0] = direct[...]
    pl.semaphore_wait(bar, len(peers))

    def gather_plus(it, du, dz):
        slot = u * 2 + z
        i = du * 2 + dz
        return copy(plus.at[it], pblk.at[it, :, pl.ds(pl.multiple_of(slot * 32, 32), 32), :],
                    ssem.at[it, i], rsem.at[it, i], ring_u(du, dz))

    def recv_plus(it, du, dz):
        slot = wrap(u - du) * 2 + lax.rem(z + dz, 2)
        i = du * 2 + dz
        return copy(plus.at[it], pblk.at[it, :, pl.ds(pl.multiple_of(slot * 32, 32), 32), :],
                    ssem.at[it, i], rsem.at[it, i], ring_u(du, dz))

    around = [(du, dz) for du in range(4) for dz in range(2) if (du, dz) != (0, 0)]

    for d in (2, 1, 3):
        send_reflection(d, 0).start()
    arrange(1)
    for d in (2, 1, 3):
        send_reflection(d, 1).start()
    partner_reflection().start()
    for du, dz in around:
        gather_plus(0, du, dz).start()
    rblk[:, :, pl.ds(pl.multiple_of(mine * 32, 32), 32), :] = rsend[c * 4 + v]

    on = onsets[...]
    for h in range(2):
        low, high = on[h * 16:h * 16 + 8], on[h * 16 + 8:h * 16 + 16]
        onw[h] = jnp.concatenate([low, low, high, high], axis=1)

    def window(xf, it, h):
        rows16 = pl.ds(h * 16, 16)
        spec = xf[it, :, :, rows16, :].reshape(32, 16, 128).astype(F32)
        both = jnp.concatenate([spec[:, :8].reshape(256, 128), spec[:, 8:].reshape(256, 128)], axis=1)
        lane = lax.rem(lax.broadcasted_iota(jnp.int32, (256, 256), 1), 128)
        real = jnp.where(lane < 64, both, 0.0).astype(BF)
        imag = jnp.where(lane < 64, 0.0, both).astype(BF)
        stacked = jnp.concatenate([real, imag], axis=0)
        traces = jnp.dot(first[...], stacked, preferred_element_type=F32).reshape(64, 8, 256)
        times = lax.broadcasted_iota(jnp.int32, (64, 8, 256), 0)
        kept = jnp.where(times < onw[h][None], traces, 0.0).astype(BF).reshape(512, 256)
        back = jnp.dot(second[fme], kept, preferred_element_type=F32)
        lane = lax.rem(lax.broadcasted_iota(jnp.int32, (64, 256), 1), 128)
        chosen = jnp.where(lane < 64, back[:64], back[64:]).reshape(8, 8, 256)
        return jnp.concatenate([chosen[:, :, :128], chosen[:, :, 128:]], axis=1)

    def gather_freq(xf, it, d, base):
        return copy(xf.at[it, fme], xf.at[it, fme], ssem.at[it, base + d], rsem.at[it, base + d], freq_on(d))

    def recv_freq(xf, it, d, base):
        g = wrap(fme - d)
        return copy(xf.at[it, g], xf.at[it, g], ssem.at[it, base + d], rsem.at[it, base + d], freq_on(d))

    def send_rows(it, d, cp):
        j = wrap(v + d) * 2 + cp
        return copy(s1.at[it, j], r1.at[it, d * 2 + c], ssem.at[it, 8 + d * 2 + cp], rsem.at[it, 8 + d * 2 + c],
                    on_ring(d, cp))

    def partner_rows(it):
        return copy(s1.at[it, v * 2 + 1 - c], r1.at[it, c], ssem.at[it, 8], rsem.at[it, 8 + c], partner)

    def recv_rows(it, d, cs):
        return copy(s1.at[it, 0], r1.at[it, d * 2 + cs], ssem.at[it, 8], rsem.at[it, 8 + d * 2 + cs], partner)

    def send_minus(it, d, cp):
        slot = (x if cp == 0 else y) * 2 + c
        return copy(minus.at[it], mblk.at[it, :, pl.ds(pl.multiple_of(slot * 32, 32), 32), :],
                    ssem.at[it, 20 + d * 2 + cp], rsem.at[it, 20 + d * 2 + c], to_ring(d, cp))

    def partner_minus(it):
        slot = jnp.where(zero, y, x) * 2 + c
        return copy(minus.at[it], mblk.at[it, :, pl.ds(pl.multiple_of(slot * 32, 32), 32), :],
                    ssem.at[it, 20], rsem.at[it, 20 + c], partner)

    def recv_minus(it, d, cs):
        slot = wrap(v - d) * 2 + cs
        return copy(minus.at[it], mblk.at[it, :, pl.ds(pl.multiple_of(slot * 32, 32), 32), :],
                    ssem.at[it, 20], rsem.at[it, 20 + d * 2 + cs], partner)

    def send_sources(it, du, dz):
        k = wrap(u + du) * 2 + lax.rem(z + dz, 2)
        i = du * 2 + dz
        return copy(s2.at[it, k], r2.at[it, i], ssem.at[it, 28 + i], rsem.at[it, 28 + i], ring_u(du, dz))

    def total(r, it, keep):
        def step(f, carry):
            acc = r[it, 0, f].astype(F32)
            for i in range(1, 8):
                acc = acc + r[it, i, f].astype(F32)
            keep[it, fme, f] = acc.astype(BF)
            return carry
        lax.fori_loop(0, 8, step, 0)

    ring = [(d, cp) for d in (2, 1, 3) for cp in range(2)]

    def iteration(it, carry):
        @pl.when(it > 0)
        def _():
            for du, dz in around:
                gather_plus(it, du, dz).start()
        own = u * 2 + z
        pblk[it, :, pl.ds(pl.multiple_of(own * 32, 32), 32), :] = plus[it]
        for du, dz in around:
            recv_plus(it, du, dz).wait_recv()

        @pl.when(it == 0)
        def _():
            for d, cs in ring:
                recv_reflection(d, cs).wait_recv()
            recv_reflection(0, 1 - c).wait_recv()

        def forward(f, carry):
            block = pblk[it, f]
            out = jnp.dot(rblk[f, 0], block, preferred_element_type=F32)
            out = out + jnp.dot(rblk[f, 1], turned(block, 1), preferred_element_type=F32)
            s1[it, :, f] = out.astype(BF).reshape(8, 32, 128)
            return carry
        lax.fori_loop(0, 8, forward, 0)
        for d, cp in ring:
            send_rows(it, d, cp).start()
        partner_rows(it).start()
        r1[it, c] = s1[it, mine]

        @pl.when(it == 0)
        def _():
            def flip(f, carry):
                for part in range(2):
                    rtrans[f, part] = rblk[f, part].T
                return carry
            lax.fori_loop(0, 8, flip, 0)

        for d, cs in ring:
            recv_rows(it, d, cs).wait_recv()
        recv_rows(it, 0, 1 - c).wait_recv()
        total(r1, it, xf1)
        for d in (2, 1, 3):
            gather_freq(xf1, it, d, 16).start()
        for d in (1, 3, 2):
            recv_freq(xf1, it, d, 16).wait_recv()
        for h in range(2):
            value = window(xf1, it, h).astype(BF)
            minus[it, :, pl.ds(h * 16, 16), :] = value
            minus_out[:, pl.ds(h * 16, 16), :] = value

        for d, cp in ring:
            send_minus(it, d, cp).start()
        partner_minus(it).start()
        mblk[it, :, pl.ds(pl.multiple_of(mine * 32, 32), 32), :] = minus[it]
        for d, cs in ring:
            recv_minus(it, d, cs).wait_recv()
        recv_minus(it, 0, 1 - c).wait_recv()

        def adjoint(f, carry):
            block = mblk[it, f]
            out = jnp.dot(rtrans[f, 0], block, preferred_element_type=F32)
            out = out + jnp.dot(rtrans[f, 1], turned(block, -1), preferred_element_type=F32)
            s2[it, :, f] = out.astype(BF).reshape(8, 32, 128)
            return carry
        lax.fori_loop(0, 8, adjoint, 0)
        for du, dz in around:
            send_sources(it, du, dz).start()
        r2[it, 0] = s2[it, own]
        for du, dz in around:
            send_sources(it, du, dz).wait_recv()
        total(r2, it, xf2)
        for d in (2, 1, 3):
            gather_freq(xf2, it, d, 36).start()
        for d in (1, 3, 2):
            recv_freq(xf2, it, d, 36).wait_recv()
        for h in range(2):
            rows16 = pl.ds(h * 16, 16)
            value = (direct[:, rows16, :].astype(F32) + window(xf2, it, h)).astype(BF)
            plus[it + 1, :, rows16, :] = value
            plus_out[:, rows16, :] = value

        for du, dz in around:
            gather_plus(it, du, dz).wait_send()
            send_sources(it, du, dz).wait_send()
        for d, cp in ring:
            send_rows(it, d, cp).wait_send()
            send_minus(it, d, cp).wait_send()
        partner_rows(it).wait_send()
        partner_minus(it).wait_send()
        for d in (1, 2, 3):
            gather_freq(xf1, it, d, 16).wait_send()
            gather_freq(xf2, it, d, 36).wait_send()
        return carry

    lax.fori_loop(0, ITERS, iteration, 0)
    for d, cp in ring:
        send_reflection(d, cp).wait_send()
    partner_reflection().wait_send()


def local(reflection, focus_direct, onsets):
    first, second = window_tables()
    block = jax.ShapeDtypeStruct((8, 32, 128), BF)
    vmem = pl.BlockSpec(memory_space=pltpu.VMEM)
    return pl.pallas_call(
        kernel,
        out_shape=(block, block),
        in_specs=[vmem] * 5,
        out_specs=(vmem, vmem),
        scratch_shapes=[
            pltpu.VMEM((8, 8, 2, 32, 256), BF),
            pltpu.VMEM((8, 2, 256, 256), BF),
            pltpu.VMEM((8, 2, 256, 256), BF),
            pltpu.VMEM((ITERS + 1, 8, 32, 128), BF),
            pltpu.VMEM((ITERS, 8, 256, 128), BF),
            pltpu.VMEM((ITERS, 8, 8, 32, 128), BF),
            pltpu.VMEM((ITERS, 8, 8, 32, 128), BF),
            pltpu.VMEM((ITERS, 4, 8, 32, 128), BF),
            pltpu.VMEM((ITERS, 8, 32, 128), BF),
            pltpu.VMEM((ITERS, 8, 256, 128), BF),
            pltpu.VMEM((ITERS, 8, 8, 32, 128), BF),
            pltpu.VMEM((ITERS, 8, 8, 32, 128), BF),
            pltpu.VMEM((ITERS, 4, 8, 32, 128), BF),
            pltpu.VMEM((2, 8, 256), jnp.int32),
            pltpu.SemaphoreType.DMA((8,)),
            pltpu.SemaphoreType.DMA((8,)),
            pltpu.SemaphoreType.DMA((ITERS, 40)),
            pltpu.SemaphoreType.DMA((ITERS, 40)),
        ],
        compiler_params=pltpu.CompilerParams(
            collective_id=0, has_side_effects=True, vmem_limit_bytes=48 * 1024 * 1024),
        name="marchenko",
    )(reflection, focus_direct, onsets, jnp.asarray(first), jnp.asarray(second))


def solution(mesh):
    in_specs = (P("freq", None, "rows", None), P("freq", "rows", None), P("rows", None))
    out_specs = (P("freq", "rows", None), P("freq", "rows", None))
    return jax.shard_map(local, mesh=mesh, in_specs=in_specs, out_specs=out_specs, check_vma=False)
```

```python
import math

import jax
import jax.numpy as jnp
import numpy as np
from jax import lax
from jax.experimental import pallas as pl
from jax.experimental.pallas import tpu as pltpu
from jax.sharding import PartitionSpec as P

NT = 128
ITERS = 2
MESH = pl.DeviceIdType.MESH
BF = jnp.bfloat16
F32 = jnp.float32
Q = 2
F = 8 // Q


def window_tables():
    t = np.arange(64)[:, None]
    k = np.arange(1, 33)[None, :]
    ang = 2.0 * np.pi * ((t * k) % NT) / NT
    parts = np.stack([np.cos(ang), np.sin(ang)])
    eye = np.eye(8)
    first = np.einsum("ctf,rs->trcfs", parts, eye).reshape(512, 512)
    weight = np.where(np.arange(64) == 0, 2.0, 4.0) / NT
    back = parts * weight[None, :, None]
    second = np.einsum("ctgqf,rs->gqcfrts", back.reshape(2, 64, 4, Q, F), eye).reshape(4, 128, 512)
    return first.astype(jnp.bfloat16), second.astype(jnp.bfloat16)


def turned(block, sign):
    real, imag = block[:, :64], block[:, 64:]
    if sign > 0:
        return jnp.concatenate([-imag, real], axis=1)
    return jnp.concatenate([imag, -real], axis=1)


def kernel(refl_hbm, direct_hbm, onsets_hbm, first_hbm, second_hbm, plus_out, minus_out,
           refl, direct, onsets, first, second,
           rsend, rblk, rtrans, plus, pblk, s1, r1, xf1, minus, mblk, s2, r2, xf2, kept, onw,
           lsem, rsnd, rrcv, ssem, rsem):
    fme = lax.axis_index("freq")
    row = lax.axis_index("rows")
    c = lax.rem(row, 2)
    x = lax.rem(row // 2, 4)
    z = lax.rem(row // 8, 2)
    y = row // 16
    zero = c == 0
    u = jnp.where(zero, y, x)
    v = jnp.where(zero, x, y)

    def rows(y, z, x, c):
        return ((y * 2 + z) * 4 + x) * 2 + c

    def wrap(a):
        return lax.rem(a + 8, 4)

    def ring_u(du, dz):
        up, zp = wrap(u + du), lax.rem(z + dz, 2)
        return (fme, jnp.where(zero, rows(up, zp, x, c), rows(y, zp, up, c)))

    def to_ring(d, cp):
        return (fme, rows(y, z, wrap(x + d), 0) if cp == 0 else rows(wrap(y + d), z, x, 1))

    def on_ring(d, cp):
        vp = wrap(v + d)
        return (fme, jnp.where(zero, rows(y, z, vp, cp), rows(vp, z, x, cp)))

    partner = (fme, rows(y, z, x, 1 - c))

    def freq_on(d):
        return (wrap(fme + d), row)

    around = [(du, dz) for du in (2, 1, 3, 0) for dz in (1, 0) if (du, dz) != (0, 0)]
    ring = [(d, cp) for d in (2, 1, 3) for cp in range(2)]

    bar = pltpu.get_barrier_semaphore()
    peers = [partner]
    peers += [ring_u(du, dz) for du, dz in around]
    peers += [to_ring(d, cp) for d, cp in ring]
    peers += [on_ring(d, cp) for d, cp in ring]
    peers += [freq_on(d) for d in range(1, 4)]
    for q in peers:
        pl.semaphore_signal(bar, inc=1, device_id=q, device_id_type=MESH)
    loads = [pltpu.make_async_copy(refl_hbm, refl, lsem.at[0]), pltpu.make_async_copy(direct_hbm, direct, lsem.at[1]),
             pltpu.make_async_copy(onsets_hbm, onsets, lsem.at[2]), pltpu.make_async_copy(first_hbm, first, lsem.at[3]),
             pltpu.make_async_copy(second_hbm.at[fme], second, lsem.at[4])]
    for load in loads:
        load.start()

    def copy(src, dst, send, recv, device):
        return pltpu.make_async_remote_copy(
            src_ref=src, dst_ref=dst, send_sem=send, recv_sem=recv, device_id=device, device_id_type=MESH)

    def pieces(cp, w):
        if cp == 0:
            return [(k * 256 + w * 64) for k in range(8)]
        return [((w * 2 + k % 2) * 256 + (k // 2) * 64 + 32) for k in range(8)]

    def arrange(q):
        def step(i, carry):
            block = refl[q * F + i].reshape(64, 2048)
            for cp in range(2):
                for w in range(4):
                    out = jnp.concatenate([block[:, p:p + 32] for p in pieces(cp, w)], axis=1)
                    rsend[q, cp * 4 + w, i] = out.reshape(2, 32, 256)
            return carry
        lax.fori_loop(0, F, step, 0)

    mine = v * 2 + c
    own = u * 2 + z

    def send_reflection(q, d, cp):
        place = x if cp == 0 else y
        return copy(rsend.at[q, cp * 4 + wrap(place + d)], rblk.at[q, place * 2 + c],
                    rsnd.at[q, d * 2 + cp], rrcv.at[q, d * 2 + c], to_ring(d, cp))

    def partner_reflection(q):
        return copy(rsend.at[q, (1 - c) * 4 + u], rblk.at[q, u * 2 + c], rsnd.at[q, 0], rrcv.at[q, c], partner)

    def recv_reflection(q, d, cs):
        return copy(rsend.at[q, 0], rblk.at[q, wrap(v - d) * 2 + cs], rsnd.at[q, 0], rrcv.at[q, d * 2 + cs], partner)

    def send_plus(it, q, du, dz):
        i = du * 2 + dz
        return copy(plus.at[it, q], pblk.at[it, q, own], ssem.at[it, q, i], rsem.at[it, q, i], ring_u(du, dz))

    def recv_plus(it, q, du, dz):
        slot = wrap(u - du) * 2 + lax.rem(z + dz, 2)
        i = du * 2 + dz
        return copy(plus.at[it, q], pblk.at[it, q, slot], ssem.at[it, q, i], rsem.at[it, q, i], ring_u(du, dz))

    def send_rows(it, q, d, cp):
        return copy(s1.at[it, q, wrap(v + d) * 2 + cp], r1.at[it, q, d * 2 + c],
                    ssem.at[it, q, 8 + d * 2 + cp], rsem.at[it, q, 8 + d * 2 + c], on_ring(d, cp))

    def partner_rows(it, q):
        return copy(s1.at[it, q, v * 2 + 1 - c], r1.at[it, q, c], ssem.at[it, q, 8], rsem.at[it, q, 8 + c], partner)

    def recv_rows(it, q, d, cs):
        return copy(s1.at[it, q, 0], r1.at[it, q, d * 2 + cs], ssem.at[it, q, 8], rsem.at[it, q, 8 + d * 2 + cs], partner)

    def send_freq(xf, it, q, d, base):
        return copy(xf.at[it, q, fme], xf.at[it, q, fme], ssem.at[it, q, base + d], rsem.at[it, q, base + d], freq_on(d))

    def recv_freq(xf, it, q, d, base):
        g = wrap(fme - d)
        return copy(xf.at[it, q, g], xf.at[it, q, g], ssem.at[it, q, base + d], rsem.at[it, q, base + d], freq_on(d))

    def send_minus(it, q, d, cp):
        place = x if cp == 0 else y
        return copy(minus.at[it, q], mblk.at[it, q, place * 2 + c],
                    ssem.at[it, q, 20 + d * 2 + cp], rsem.at[it, q, 20 + d * 2 + c], to_ring(d, cp))

    def partner_minus(it, q):
        return copy(minus.at[it, q], mblk.at[it, q, u * 2 + c], ssem.at[it, q, 20], rsem.at[it, q, 20 + c], partner)

    def recv_minus(it, q, d, cs):
        return copy(minus.at[it, q], mblk.at[it, q, wrap(v - d) * 2 + cs],
                    ssem.at[it, q, 20], rsem.at[it, q, 20 + d * 2 + cs], partner)

    def send_sources(it, q, du, dz):
        i = du * 2 + dz
        return copy(s2.at[it, q, wrap(u + du) * 2 + lax.rem(z + dz, 2)], r2.at[it, q, i],
                    ssem.at[it, q, 28 + i], rsem.at[it, q, 28 + i], ring_u(du, dz))

    loads[1].wait()
    for q in range(Q):
        plus[0, q] = direct[q * F:(q + 1) * F]
    loads[0].wait()
    for q in range(Q):
        arrange(q)
        if q == 0:
            pl.semaphore_wait(bar, len(peers))
        for d, cp in ring:
            send_reflection(q, d, cp).start()
        partner_reflection(q).start()
        for du, dz in around:
            send_plus(0, q, du, dz).start()
        rblk[q, mine] = rsend[q, c * 4 + v]

    loads[2].wait()
    on = onsets[...]
    for h in range(2):
        low, high = on[h * 16:h * 16 + 8], on[h * 16 + 8:h * 16 + 16]
        onw[h] = jnp.concatenate([low, low, high, high], axis=1)
    loads[3].wait()
    loads[4].wait()

    def window_in(xf, it):
        for h in range(2):
            spec = [xf[it, q, g, :, h * 16:(h + 1) * 16, :] for g in range(4) for q in range(Q)]
            spec = jnp.concatenate(spec, axis=0).astype(F32)
            both = jnp.concatenate([spec[:, :8].reshape(256, 128), spec[:, 8:].reshape(256, 128)], axis=1)
            lane = lax.rem(lax.broadcasted_iota(jnp.int32, (256, 256), 1), 128)
            real = jnp.where(lane < 64, both, 0.0).astype(BF)
            imag = jnp.where(lane < 64, 0.0, both).astype(BF)
            stacked = jnp.concatenate([real, imag], axis=0)
            traces = jnp.dot(first[...], stacked, preferred_element_type=F32).reshape(64, 8, 256)
            times = lax.broadcasted_iota(jnp.int32, (64, 8, 256), 0)
            kept[h] = jnp.where(times < onw[h][None], traces, 0.0).astype(BF).reshape(512, 256)

    def window_out(q, h):
        back = jnp.dot(second[q * 16 * F:(q + 1) * 16 * F], kept[h], preferred_element_type=F32)
        lane = lax.rem(lax.broadcasted_iota(jnp.int32, (8 * F, 256), 1), 128)
        chosen = jnp.where(lane < 64, back[:8 * F], back[8 * F:]).reshape(F, 8, 256)
        return jnp.concatenate([chosen[:, :, :128], chosen[:, :, 128:]], axis=1)

    def total(r, it, q, keep):
        def step(f, carry):
            acc = r[it, q, 0, f].astype(F32)
            for i in range(1, 8):
                acc = acc + r[it, q, i, f].astype(F32)
            keep[it, q, fme, f] = acc.astype(BF)
            return carry
        lax.fori_loop(0, F, step, 0, unroll=True)

    def iteration(it, carry):
        for q in range(Q):
            pblk[it, q, own] = plus[it, q]
        for q in range(Q):
            for du, dz in around:
                recv_plus(it, q, du, dz).wait_recv()

            @pl.when(it == 0)
            def _():
                for d, cs in ring:
                    recv_reflection(q, d, cs).wait_recv()
                recv_reflection(q, 0, 1 - c).wait_recv()

            def forward(i, carry):
                block = pblk[it, q, :, i].reshape(256, 128)
                out = jnp.dot(rblk[q, :, i, 0].reshape(256, 256), block, preferred_element_type=F32)
                out = out + jnp.dot(rblk[q, :, i, 1].reshape(256, 256), turned(block, 1), preferred_element_type=F32)
                s1[it, q, :, i] = out.astype(BF).reshape(8, 32, 128)
                return carry
            lax.fori_loop(0, F, forward, 0, unroll=True)
            for d, cp in ring:
                send_rows(it, q, d, cp).start()
            partner_rows(it, q).start()
            r1[it, q, c] = s1[it, q, mine]

        @pl.when(it == 0)
        def _():
            for q in range(Q):
                def flip(i, carry):
                    for part in range(2):
                        rtrans[q * F + i, part] = rblk[q, :, i, part].reshape(256, 256).T
                    return carry
                lax.fori_loop(0, F, flip, 0)

        for q in range(Q):
            for d, cs in ring:
                recv_rows(it, q, d, cs).wait_recv()
            recv_rows(it, q, 0, 1 - c).wait_recv()
            total(r1, it, q, xf1)
            for d in (2, 1, 3):
                send_freq(xf1, it, q, d, 16).start()
        for q in range(Q):
            for d in (1, 3, 2):
                recv_freq(xf1, it, q, d, 16).wait_recv()
        window_in(xf1, it)

        for q in range(Q):
            for h in range(2):
                value = window_out(q, h).astype(BF)
                minus[it, q, :, h * 16:(h + 1) * 16, :] = value
                minus_out[q * F:(q + 1) * F, h * 16:(h + 1) * 16, :] = value
            for d, cp in ring:
                send_minus(it, q, d, cp).start()
            partner_minus(it, q).start()
            mblk[it, q, mine] = minus[it, q]
        for q in range(Q):
            for d, cs in ring:
                recv_minus(it, q, d, cs).wait_recv()
            recv_minus(it, q, 0, 1 - c).wait_recv()

            def adjoint(i, carry):
                block = mblk[it, q, :, i].reshape(256, 128)
                out = jnp.dot(rtrans[q * F + i, 0], block, preferred_element_type=F32)
                out = out + jnp.dot(rtrans[q * F + i, 1], turned(block, -1), preferred_element_type=F32)
                s2[it, q, :, i] = out.astype(BF).reshape(8, 32, 128)
                return carry
            lax.fori_loop(0, F, adjoint, 0, unroll=True)
            for du, dz in around:
                send_sources(it, q, du, dz).start()
            r2[it, q, 0] = s2[it, q, own]
        for q in range(Q):
            for du, dz in around:
                send_sources(it, q, du, dz).wait_recv()
            total(r2, it, q, xf2)
            for d in (2, 1, 3):
                send_freq(xf2, it, q, d, 36).start()
        for q in range(Q):
            for d in (1, 3, 2):
                recv_freq(xf2, it, q, d, 36).wait_recv()
        window_in(xf2, it)
        for q in range(Q):
            for h in range(2):
                rows16 = slice(h * 16, (h + 1) * 16)
                value = (direct[q * F:(q + 1) * F, rows16, :].astype(F32) + window_out(q, h)).astype(BF)
                plus[it + 1, q, :, rows16, :] = value
                plus_out[q * F:(q + 1) * F, rows16, :] = value

            @pl.when(it + 1 < ITERS)
            def _():
                for du, dz in around:
                    send_plus(it + 1, q, du, dz).start()

        for q in range(Q):
            for du, dz in around:
                send_plus(it, q, du, dz).wait_send()
                send_sources(it, q, du, dz).wait_send()
            for d, cp in ring:
                send_rows(it, q, d, cp).wait_send()
                send_minus(it, q, d, cp).wait_send()
            partner_rows(it, q).wait_send()
            partner_minus(it, q).wait_send()
            for d in (1, 2, 3):
                send_freq(xf1, it, q, d, 16).wait_send()
                send_freq(xf2, it, q, d, 36).wait_send()
        return carry

    lax.fori_loop(0, ITERS, iteration, 0)
    for q in range(Q):
        for d, cp in ring:
            send_reflection(q, d, cp).wait_send()
        partner_reflection(q).wait_send()


def local(reflection, focus_direct, onsets):
    first, second = window_tables()
    block = jax.ShapeDtypeStruct((8, 32, 128), BF)
    vmem = pl.BlockSpec(memory_space=pltpu.VMEM)
    part = (F, 32, 128)
    return pl.pallas_call(
        kernel,
        out_shape=(block, block),
        in_specs=[pl.BlockSpec(memory_space=pl.ANY)] * 5,
        out_specs=(vmem, vmem),
        scratch_shapes=[
            pltpu.VMEM((8, 2, 32, 2048), BF),
            pltpu.VMEM((8, 32, 128), BF),
            pltpu.VMEM((32, 64), jnp.int32),
            pltpu.VMEM((512, 512), BF),
            pltpu.VMEM((128, 512), BF),
            pltpu.VMEM((Q, 8, F, 2, 32, 256), BF),
            pltpu.VMEM((Q, 8, F, 2, 32, 256), BF),
            pltpu.VMEM((8, 2, 256, 256), BF),
            pltpu.VMEM((ITERS + 1, Q) + part, BF),
            pltpu.VMEM((ITERS, Q, 8) + part, BF),
            pltpu.VMEM((ITERS, Q, 8) + part, BF),
            pltpu.VMEM((ITERS, Q, 8) + part, BF),
            pltpu.VMEM((ITERS, Q, 4) + part, BF),
            pltpu.VMEM((ITERS, Q) + part, BF),
            pltpu.VMEM((ITERS, Q, 8) + part, BF),
            pltpu.VMEM((ITERS, Q, 8) + part, BF),
            pltpu.VMEM((ITERS, Q, 8) + part, BF),
            pltpu.VMEM((ITERS, Q, 4) + part, BF),
            pltpu.VMEM((2, 512, 256), BF),
            pltpu.VMEM((2, 8, 256), jnp.int32),
            pltpu.SemaphoreType.DMA((5,)),
            pltpu.SemaphoreType.DMA((Q, 8)),
            pltpu.SemaphoreType.DMA((Q, 8)),
            pltpu.SemaphoreType.DMA((ITERS, Q, 40)),
            pltpu.SemaphoreType.DMA((ITERS, Q, 40)),
        ],
        compiler_params=pltpu.CompilerParams(
            collective_id=0, has_side_effects=True, vmem_limit_bytes=60 * 1024 * 1024),
        name="marchenko",
    )(reflection, focus_direct, onsets, jnp.asarray(first), jnp.asarray(second))


def solution(mesh):
    in_specs = (P("freq", None, "rows", None), P("freq", "rows", None), P("rows", None))
    out_specs = (P("freq", "rows", None), P("freq", "rows", None))
    return jax.shard_map(local, mesh=mesh, in_specs=in_specs, out_specs=out_specs, check_vma=False)
```

```python
import math

import jax
import jax.numpy as jnp
import numpy as np
from jax import lax
from jax.experimental import pallas as pl
from jax.experimental.pallas import tpu as pltpu
from jax.sharding import PartitionSpec as P

NT = 128
ITERS = 2
MESH = pl.DeviceIdType.MESH
BF = jnp.bfloat16
F32 = jnp.float32
Q = 2
CHAINS = 2
S = CHAINS * Q
R4 = 4 // Q
F = 8 // Q


def window_tables():
    t = np.arange(64)[:, None]
    k = np.arange(1, 33)[None, :]
    ang = 2.0 * np.pi * ((t * k) % NT) / NT
    parts = np.stack([np.cos(ang), np.sin(ang)])
    eye = np.eye(8)
    paired = parts.reshape(2, 64, 4, Q, R4, 2)
    first = np.einsum("ctgqfo,rs->trcoqgfs", paired, eye).reshape(512, 512)
    weight = np.where(np.arange(64) == 0, 2.0, 4.0) / NT
    back = paired * weight[None, :, None, None, None, None]
    second = np.einsum("ctgqfo,rs->gcoqfrts", back, eye).reshape(4, 128, 512)
    return first.astype(jnp.bfloat16), second.astype(jnp.bfloat16)


def turned(block, sign):
    p = [block[:, 32 * i:32 * i + 32] for i in range(4)]
    if sign > 0:
        return jnp.concatenate([-p[1], p[0], -p[3], p[2]], axis=1)
    return jnp.concatenate([p[1], -p[0], p[3], -p[2]], axis=1)


def kernel(refl_hbm, direct_hbm, onsets_hbm, first_hbm, second_hbm, plus_out, minus_out,
           refl, direct, onsets, first, second,
           rsend, rblk, rtrans, plus, pblk, s1, r1, xf1, minus, mblk, s2, r2, xf2, kept, onw, packed,
           lsem, rsnd, rrcv, ssem, rsem):
    fme = lax.axis_index("freq")
    row = lax.axis_index("rows")
    c = lax.rem(row, 2)
    x = lax.rem(row // 2, 4)
    z = lax.rem(row // 8, 2)
    y = row // 16
    zero = c == 0
    u = jnp.where(zero, y, x)
    v = jnp.where(zero, x, y)

    def rows(y, z, x, c):
        return ((y * 2 + z) * 4 + x) * 2 + c

    def wrap(a):
        return lax.rem(a + 8, 4)

    def ring_u(du, dz):
        up, zp = wrap(u + du), lax.rem(z + dz, 2)
        return (fme, jnp.where(zero, rows(up, zp, x, c), rows(y, zp, up, c)))

    def to_ring(d, cp):
        return (fme, rows(y, z, wrap(x + d), 0) if cp == 0 else rows(wrap(y + d), z, x, 1))

    def on_ring(d, cp):
        vp = wrap(v + d)
        return (fme, jnp.where(zero, rows(y, z, vp, cp), rows(vp, z, x, cp)))

    partner = (fme, rows(y, z, x, 1 - c))

    def freq_on(d):
        return (wrap(fme + d), row)

    around = [(du, dz) for du in (2, 1, 3, 0) for dz in (1, 0) if (du, dz) != (0, 0)]
    ring = [(d, cp) for d in (2, 1, 3) for cp in range(2)]

    bar = pltpu.get_barrier_semaphore()
    peers = [partner]
    peers += [ring_u(du, dz) for du, dz in around]
    peers += [to_ring(d, cp) for d, cp in ring]
    peers += [on_ring(d, cp) for d, cp in ring]
    peers += [freq_on(d) for d in range(1, 4)]
    for q in peers:
        pl.semaphore_signal(bar, inc=1, device_id=q, device_id_type=MESH)
    loads = [pltpu.make_async_copy(refl_hbm, refl, lsem.at[0]), pltpu.make_async_copy(direct_hbm, direct, lsem.at[1]),
             pltpu.make_async_copy(onsets_hbm, onsets, lsem.at[2]), pltpu.make_async_copy(first_hbm, first, lsem.at[3]),
             pltpu.make_async_copy(second_hbm.at[fme], second, lsem.at[4])]
    for load in loads:
        load.start()

    def copy(src, dst, send, recv, device):
        return pltpu.make_async_remote_copy(
            src_ref=src, dst_ref=dst, send_sem=send, recv_sem=recv, device_id=device, device_id_type=MESH)

    def pieces(cp, w):
        if cp == 0:
            return [(k * 256 + w * 64) for k in range(8)]
        return [((w * 2 + k % 2) * 256 + (k // 2) * 64 + 32) for k in range(8)]

    def arrange(q):
        def step(i, carry):
            block = refl[q * F + i].reshape(64, 2048)
            for cp in range(2):
                for w in range(4):
                    out = jnp.concatenate([block[:, p:p + 32] for p in pieces(cp, w)], axis=1)
                    rsend[q, cp * 4 + w, i] = out.reshape(2, 32, 256)
            return carry
        lax.fori_loop(0, F, step, 0)

    mine = v * 2 + c
    own = u * 2 + z

    def send_reflection(q, d, cp):
        place = x if cp == 0 else y
        return copy(rsend.at[q, cp * 4 + wrap(place + d)], rblk.at[q, place * 2 + c],
                    rsnd.at[q], rrcv.at[q], to_ring(d, cp))

    def partner_reflection(q):
        return copy(rsend.at[q, (1 - c) * 4 + u], rblk.at[q, u * 2 + c], rsnd.at[q], rrcv.at[q], partner)

    def wait_for(buffer, count, send, recv):
        return copy(buffer.at[pl.ds(0, count)], buffer.at[pl.ds(0, count)], send, recv, partner)

    def all_reflection(q):
        return wait_for(rblk.at[q], 7, rsnd.at[q], rrcv.at[q])

    def stage(it, q, n):
        return ssem.at[it, q, n], rsem.at[it, q, n]

    def send_plus(it, q, du, dz):
        return copy(plus.at[it, q], pblk.at[it, q, own], *stage(it, q, 0), ring_u(du, dz))

    def all_plus(it, q):
        return wait_for(pblk.at[it, q], 7, *stage(it, q, 0))

    def send_rows(it, q, d, cp):
        return copy(s1.at[it, q, wrap(v + d) * 2 + cp], r1.at[it, q, d * 2 + c], *stage(it, q, 1), on_ring(d, cp))

    def partner_rows(it, q):
        return copy(s1.at[it, q, v * 2 + 1 - c], r1.at[it, q, c], *stage(it, q, 1), partner)

    def all_rows(it, q):
        return wait_for(r1.at[it, q], 7, *stage(it, q, 1))

    def send_freq(xf, it, q, d, n):
        return copy(xf.at[it, q, fme], xf.at[it, q, fme], *stage(it, q, n), freq_on(d))

    def all_freq(xf, it, q, n):
        return wait_for(xf.at[it, q], 3, *stage(it, q, n))

    def send_minus(it, q, d, cp):
        place = x if cp == 0 else y
        return copy(minus.at[it, q], mblk.at[it, q, place * 2 + c], *stage(it, q, 3), to_ring(d, cp))

    def partner_minus(it, q):
        return copy(minus.at[it, q], mblk.at[it, q, u * 2 + c], *stage(it, q, 3), partner)

    def all_minus(it, q):
        return wait_for(mblk.at[it, q], 7, *stage(it, q, 3))

    def send_sources(it, q, du, dz):
        i = du * 2 + dz
        return copy(s2.at[it, q, wrap(u + du) * 2 + lax.rem(z + dz, 2)], r2.at[it, q, i], *stage(it, q, 4), ring_u(du, dz))

    def all_sources(it, q):
        return wait_for(r2.at[it, q], 7, *stage(it, q, 4))

    loads[1].wait()
    for s in range(S):
        h, q = s // Q, s % Q
        for i in range(R4):
            pair = [direct[q * F + 2 * i + o] for o in range(2)]
            value = jnp.concatenate([pair[o][:, e:e + 32] for o in range(2) for e in (32 * h, 64 + 32 * h)], axis=1)
            packed[s, i] = value
            plus[0, s, i] = value
    loads[0].wait()
    for q in range(Q):
        arrange(q)
        if q == 0:
            pl.semaphore_wait(bar, len(peers))
        for d, cp in ring:
            send_reflection(q, d, cp).start()
        partner_reflection(q).start()
        for h in range(CHAINS):
            for du, dz in around:
                send_plus(0, h * Q + q, du, dz).start()
        rblk[q, mine] = rsend[q, c * 4 + v]

    loads[2].wait()
    on = onsets[...]
    for h in range(CHAINS):
        eight = [on[8 * a:8 * a + 8, 32 * h:32 * h + 32] for a in range(4)]
        onw[h] = jnp.concatenate([eight[a] for a in range(4) for _ in range(2)], axis=1)
    loads[3].wait()
    loads[4].wait()

    def window_in(xf, it, h):
        spec = jnp.concatenate([xf[it, h * Q + q].reshape(4 * R4, 32, 128) for q in range(Q)], axis=0).astype(F32)
        odd = [jnp.concatenate([spec[:, 8 * a:8 * a + 8, 64 * o:64 * o + 64] for a in range(4)], axis=2) for o in range(2)]
        both = jnp.concatenate([odd[0].reshape(128, 256), odd[1].reshape(128, 256)], axis=0)
        lane = lax.rem(lax.broadcasted_iota(jnp.int32, (256, 256), 1), 64)
        real = jnp.where(lane < 32, both, 0.0).astype(BF)
        imag = jnp.where(lane < 32, 0.0, both).astype(BF)
        stacked = jnp.concatenate([real, imag], axis=0)
        traces = jnp.dot(first[...], stacked, preferred_element_type=F32).reshape(64, 8, 256)
        times = lax.broadcasted_iota(jnp.int32, (64, 8, 256), 0)
        kept[h] = jnp.where(times < onw[h][None], traces, 0.0).astype(BF).reshape(512, 256)

    def window_out(h):
        back = jnp.dot(second[...], kept[h], preferred_element_type=F32)
        lane = lax.rem(lax.broadcasted_iota(jnp.int32, (64, 256), 1), 64)
        chosen = jnp.where(lane < 32, back[:64], back[64:]).reshape(2, 4, 8, 256)
        return jnp.concatenate(
            [jnp.concatenate([chosen[0, :, :, 64 * a:64 * a + 64], chosen[1, :, :, 64 * a:64 * a + 64]], axis=2)
             for a in range(4)], axis=1)

    def unpack(source, out):
        for q in range(Q):
            for i in range(R4):
                for o in range(2):
                    out[q * F + 2 * i + o] = jnp.concatenate(
                        [source[h * Q + q, i][:, 64 * o + 32 * e:64 * o + 32 * e + 32] for e in range(2) for h in range(CHAINS)],
                        axis=1)

    def total(r, it, q, keep):
        def step(f, carry):
            acc = r[it, q, 0, f].astype(F32)
            for i in range(1, 8):
                acc = acc + r[it, q, i, f].astype(F32)
            keep[it, q, fme, f] = acc.astype(BF)
            return carry
        lax.fori_loop(0, R4, step, 0, unroll=True)

    low = lax.broadcasted_iota(jnp.int32, (256, 128), 1) < 64

    def iteration(it, carry):
        for s in range(S):
            pblk[it, s, own] = plus[it, s]
        for s in range(S):
            q = s % Q
            all_plus(it, s).wait_recv()

            if s < Q:
                @pl.when(it == 0)
                def _():
                    all_reflection(q).wait_recv()

            def forward(i, carry):
                block = pblk[it, s, :, i].reshape(256, 128)
                other = turned(block, 1)
                out = [jnp.dot(rblk[q, :, 2 * i + o, 0].reshape(256, 256), block, preferred_element_type=F32)
                       + jnp.dot(rblk[q, :, 2 * i + o, 1].reshape(256, 256), other, preferred_element_type=F32)
                       for o in range(2)]
                s1[it, s, :, i] = jnp.where(low, out[0], out[1]).astype(BF).reshape(8, 32, 128)
                return carry
            lax.fori_loop(0, R4, forward, 0, unroll=True)
            for d, cp in ring:
                send_rows(it, s, d, cp).start()
            partner_rows(it, s).start()
            r1[it, s, c] = s1[it, s, mine]

        @pl.when(it == 0)
        def _():
            for q in range(Q):
                def flip(i, carry):
                    for part in range(2):
                        rtrans[q * F + i, part] = rblk[q, :, i, part].reshape(256, 256).T
                    return carry
                lax.fori_loop(0, F, flip, 0)

        for s in range(S):
            all_rows(it, s).wait_recv()
            total(r1, it, s, xf1)
            for d in (2, 1, 3):
                send_freq(xf1, it, s, d, 2).start()

        for h in range(CHAINS):
            for s in range(h * Q, h * Q + Q):
                all_freq(xf1, it, s, 2).wait_recv()
            window_in(xf1, it, h)
            value = window_out(h).astype(BF)
            for q in range(Q):
                s = h * Q + q
                minus[it, s] = value[q * R4:(q + 1) * R4]
                for d, cp in ring:
                    send_minus(it, s, d, cp).start()
                partner_minus(it, s).start()
                mblk[it, s, mine] = minus[it, s]
        for s in range(S):
            q = s % Q
            all_minus(it, s).wait_recv()

            def adjoint(i, carry):
                block = mblk[it, s, :, i].reshape(256, 128)
                other = turned(block, -1)
                out = [jnp.dot(rtrans[q * F + 2 * i + o, 0], block, preferred_element_type=F32)
                       + jnp.dot(rtrans[q * F + 2 * i + o, 1], other, preferred_element_type=F32)
                       for o in range(2)]
                s2[it, s, :, i] = jnp.where(low, out[0], out[1]).astype(BF).reshape(8, 32, 128)
                return carry
            lax.fori_loop(0, R4, adjoint, 0, unroll=True)
            for du, dz in around:
                send_sources(it, s, du, dz).start()
            r2[it, s, 0] = s2[it, s, own]
        for s in range(S):
            all_sources(it, s).wait_recv()
            total(r2, it, s, xf2)
            for d in (2, 1, 3):
                send_freq(xf2, it, s, d, 5).start()
        for h in range(CHAINS):
            for s in range(h * Q, h * Q + Q):
                all_freq(xf2, it, s, 5).wait_recv()
            window_in(xf2, it, h)
            value = window_out(h)
            for q in range(Q):
                s = h * Q + q
                plus[it + 1, s] = (packed[s].astype(F32) + value[q * R4:(q + 1) * R4]).astype(BF)

                @pl.when(it + 1 < ITERS)
                def _():
                    for du, dz in around:
                        send_plus(it + 1, s, du, dz).start()

        for s in range(S):
            for copies in (all_plus(it, s), all_rows(it, s), all_freq(xf1, it, s, 2), all_minus(it, s),
                           all_sources(it, s), all_freq(xf2, it, s, 5)):
                copies.wait_send()
        return carry

    lax.fori_loop(0, ITERS, iteration, 0)
    unpack(minus.at[ITERS - 1], minus_out)
    unpack(plus.at[ITERS], plus_out)
    for q in range(Q):
        all_reflection(q).wait_send()


def local(reflection, focus_direct, onsets):
    first, second = window_tables()
    block = jax.ShapeDtypeStruct((8, 32, 128), BF)
    vmem = pl.BlockSpec(memory_space=pltpu.VMEM)
    part = (R4, 32, 128)
    return pl.pallas_call(
        kernel,
        out_shape=(block, block),
        in_specs=[pl.BlockSpec(memory_space=pl.ANY)] * 5,
        out_specs=(vmem, vmem),
        scratch_shapes=[
            pltpu.VMEM((8, 2, 32, 2048), BF),
            pltpu.VMEM((8, 32, 128), BF),
            pltpu.VMEM((32, 64), jnp.int32),
            pltpu.VMEM((512, 512), BF),
            pltpu.VMEM((128, 512), BF),
            pltpu.VMEM((Q, 8, F, 2, 32, 256), BF),
            pltpu.VMEM((Q, 8, F, 2, 32, 256), BF),
            pltpu.VMEM((8, 2, 256, 256), BF),
            pltpu.VMEM((ITERS + 1, S) + part, BF),
            pltpu.VMEM((ITERS, S, 8) + part, BF),
            pltpu.VMEM((ITERS, S, 8) + part, BF),
            pltpu.VMEM((ITERS, S, 8) + part, BF),
            pltpu.VMEM((ITERS, S, 4) + part, BF),
            pltpu.VMEM((ITERS, S) + part, BF),
            pltpu.VMEM((ITERS, S, 8) + part, BF),
            pltpu.VMEM((ITERS, S, 8) + part, BF),
            pltpu.VMEM((ITERS, S, 8) + part, BF),
            pltpu.VMEM((ITERS, S, 4) + part, BF),
            pltpu.VMEM((2, 512, 256), BF),
            pltpu.VMEM((2, 8, 256), jnp.int32),
            pltpu.VMEM((S,) + part, BF),
            pltpu.SemaphoreType.DMA((5,)),
            pltpu.SemaphoreType.DMA((Q,)),
            pltpu.SemaphoreType.DMA((Q,)),
            pltpu.SemaphoreType.DMA((ITERS, S, 6)),
            pltpu.SemaphoreType.DMA((ITERS, S, 6)),
        ],
        compiler_params=pltpu.CompilerParams(
            collective_id=0, has_side_effects=True, vmem_limit_bytes=60 * 1024 * 1024),
        name="marchenko",
    )(reflection, focus_direct, onsets, jnp.asarray(first), jnp.asarray(second))


def solution(mesh):
    in_specs = (P("freq", None, "rows", None), P("freq", "rows", None), P("rows", None))
    out_specs = (P("freq", "rows", None), P("freq", "rows", None))
    return jax.shard_map(local, mesh=mesh, in_specs=in_specs, out_specs=out_specs, check_vma=False)
```

```python
import math

import jax
import jax.numpy as jnp
import numpy as np
from jax import lax
from jax.experimental import pallas as pl
from jax.experimental.pallas import tpu as pltpu
from jax.sharding import PartitionSpec as P

NT = 128
ITERS = 2
MESH = pl.DeviceIdType.MESH
BF = jnp.bfloat16
F32 = jnp.float32
Q = 2
CHAINS = 2
S = CHAINS * Q
R4 = 4 // Q
F = 8 // Q


def window_tables():
    t = np.arange(64)[:, None]
    k = np.arange(1, 33)[None, :]
    ang = 2.0 * np.pi * ((t * k) % NT) / NT
    parts = np.stack([np.cos(ang), np.sin(ang)])
    eye = np.eye(8)
    paired = parts.reshape(2, 64, 4, Q, R4, 2)
    first = np.einsum("ctgqfo,rs->trcoqgfs", paired, eye).reshape(512, 512)
    weight = np.where(np.arange(64) == 0, 2.0, 4.0) / NT
    back = paired * weight[None, :, None, None, None, None]
    second = np.einsum("ctgqfo,rs->gcoqfrts", back, eye).reshape(4, 128, 512)
    return first.astype(jnp.bfloat16), second.astype(jnp.bfloat16)


def turned(block, sign):
    p = [block[:, 32 * i:32 * i + 32] for i in range(4)]
    if sign > 0:
        return jnp.concatenate([-p[1], p[0], -p[3], p[2]], axis=1)
    return jnp.concatenate([p[1], -p[0], p[3], -p[2]], axis=1)


def kernel(refl_hbm, direct_hbm, onsets_hbm, first_hbm, second_hbm, plus_out, minus_out,
           refl, direct, onsets, first, second,
           rsend, rblk, rtrans, plus, pblk, s1, r1, xf1, minus, mblk, s2, r2, xf2, kept, onw, packed,
           lsem, rsnd, rrcv, ssem, rsem):
    fme = lax.axis_index("freq")
    row = lax.axis_index("rows")
    c = lax.rem(row, 2)
    x = lax.rem(row // 2, 4)
    z = lax.rem(row // 8, 2)
    y = row // 16
    zero = c == 0
    u = jnp.where(zero, y, x)
    v = jnp.where(zero, x, y)

    def rows(y, z, x, c):
        return ((y * 2 + z) * 4 + x) * 2 + c

    def wrap(a):
        return lax.rem(a + 8, 4)

    def ring_u(du, dz):
        up, zp = wrap(u + du), lax.rem(z + dz, 2)
        return (fme, jnp.where(zero, rows(up, zp, x, c), rows(y, zp, up, c)))

    def to_ring(d, cp):
        return (fme, rows(y, z, wrap(x + d), 0) if cp == 0 else rows(wrap(y + d), z, x, 1))

    def on_ring(d, cp):
        vp = wrap(v + d)
        return (fme, jnp.where(zero, rows(y, z, vp, cp), rows(vp, z, x, cp)))

    partner = (fme, rows(y, z, x, 1 - c))

    def freq_on(d):
        return (wrap(fme + d), row)

    around = [(du, dz) for du in (2, 1, 3, 0) for dz in (1, 0) if (du, dz) != (0, 0)]
    ring = [(d, cp) for d in (2, 1, 3) for cp in range(2)]

    bar = pltpu.get_barrier_semaphore()
    peers = [partner]
    peers += [ring_u(du, dz) for du, dz in around]
    peers += [to_ring(d, cp) for d, cp in ring]
    peers += [on_ring(d, cp) for d, cp in ring]
    peers += [freq_on(d) for d in range(1, 4)]
    for q in peers:
        pl.semaphore_signal(bar, inc=1, device_id=q, device_id_type=MESH)
    loads = [pltpu.make_async_copy(refl_hbm, refl, lsem.at[0]), pltpu.make_async_copy(direct_hbm, direct, lsem.at[1]),
             pltpu.make_async_copy(onsets_hbm, onsets, lsem.at[2]), pltpu.make_async_copy(first_hbm, first, lsem.at[3]),
             pltpu.make_async_copy(second_hbm.at[fme], second, lsem.at[4])]
    for load in loads:
        load.start()

    def copy(src, dst, send, recv, device):
        return pltpu.make_async_remote_copy(
            src_ref=src, dst_ref=dst, send_sem=send, recv_sem=recv, device_id=device, device_id_type=MESH)

    def pieces(cp, w):
        if cp == 0:
            return [(k * 256 + w * 64) for k in range(8)]
        return [((w * 2 + k % 2) * 256 + (k // 2) * 64 + 32) for k in range(8)]

    def arrange(q):
        def step(i, carry):
            block = refl[q * F + i].reshape(64, 2048)
            for cp in range(2):
                for w in range(4):
                    out = jnp.concatenate([block[:, p:p + 32] for p in pieces(cp, w)], axis=1)
                    rsend[q, cp * 4 + w, i] = out.reshape(2, 32, 256)
            return carry
        lax.fori_loop(0, F, step, 0)

    mine = v * 2 + c
    own = u * 2 + z

    def send_reflection(q, d, cp):
        place = x if cp == 0 else y
        return copy(rsend.at[q, cp * 4 + wrap(place + d)], rblk.at[q, place * 2 + c],
                    rsnd.at[q], rrcv.at[q], to_ring(d, cp))

    def partner_reflection(q):
        return copy(rsend.at[q, (1 - c) * 4 + u], rblk.at[q, u * 2 + c], rsnd.at[q], rrcv.at[q], partner)

    def wait_for(buffer, count, send, recv):
        return copy(buffer.at[pl.ds(0, count)], buffer.at[pl.ds(0, count)], send, recv, partner)

    def all_reflection(q):
        return wait_for(rblk.at[q], 7, rsnd.at[q], rrcv.at[q])

    def stage(it, q, n):
        return ssem.at[it, q, n], rsem.at[it, q, n]

    def send_plus(it, q, du, dz):
        return copy(plus.at[it, q], pblk.at[it, q, own], *stage(it, q, 0), ring_u(du, dz))

    def all_plus(it, q):
        return wait_for(pblk.at[it, q], 7, *stage(it, q, 0))

    def send_rows(it, q, d, cp):
        return copy(s1.at[it, q, wrap(v + d) * 2 + cp], r1.at[it, q, d * 2 + c], *stage(it, q, 1), on_ring(d, cp))

    def partner_rows(it, q):
        return copy(s1.at[it, q, v * 2 + 1 - c], r1.at[it, q, c], *stage(it, q, 1), partner)

    def all_rows(it, q):
        return wait_for(r1.at[it, q], 7, *stage(it, q, 1))

    def send_freq(xf, it, q, d, n):
        return copy(xf.at[it, q, fme], xf.at[it, q, fme], *stage(it, q, n), freq_on(d))

    def all_freq(xf, it, q, n):
        return wait_for(xf.at[it, q], 3, *stage(it, q, n))

    def send_minus(it, q, d, cp):
        place = x if cp == 0 else y
        return copy(minus.at[it, q], mblk.at[it, q, place * 2 + c], *stage(it, q, 3), to_ring(d, cp))

    def partner_minus(it, q):
        return copy(minus.at[it, q], mblk.at[it, q, u * 2 + c], *stage(it, q, 3), partner)

    def all_minus(it, q):
        return wait_for(mblk.at[it, q], 7, *stage(it, q, 3))

    def send_sources(it, q, du, dz):
        i = du * 2 + dz
        return copy(s2.at[it, q, wrap(u + du) * 2 + lax.rem(z + dz, 2)], r2.at[it, q, i], *stage(it, q, 4), ring_u(du, dz))

    def all_sources(it, q):
        return wait_for(r2.at[it, q], 7, *stage(it, q, 4))

    loads[1].wait()
    for s in range(S):
        h, q = s // Q, s % Q
        for i in range(R4):
            pair = [direct[q * F + 2 * i + o] for o in range(2)]
            value = jnp.concatenate([pair[o][:, e:e + 32] for o in range(2) for e in (32 * h, 64 + 32 * h)], axis=1)
            packed[s, i] = value
            plus[0, s, i] = value
    loads[0].wait()
    for q in range(Q):
        arrange(q)
        if q == 0:
            pl.semaphore_wait(bar, len(peers))
        for d, cp in ring:
            send_reflection(q, d, cp).start()
        partner_reflection(q).start()
        for h in range(CHAINS):
            for du, dz in around:
                send_plus(0, h * Q + q, du, dz).start()
        rblk[q, mine] = rsend[q, c * 4 + v]

    loads[2].wait()
    on = onsets[...]
    for h in range(CHAINS):
        eight = [on[8 * a:8 * a + 8, 32 * h:32 * h + 32] for a in range(4)]
        onw[h] = jnp.concatenate([eight[a] for a in range(4) for _ in range(2)], axis=1)
    loads[3].wait()
    loads[4].wait()

    def window_in(xf, it, h):
        spec = jnp.concatenate([xf[it, h * Q + q].reshape(4 * R4, 32, 128) for q in range(Q)], axis=0).astype(F32)
        odd = [jnp.concatenate([spec[:, 8 * a:8 * a + 8, 64 * o:64 * o + 64] for a in range(4)], axis=2) for o in range(2)]
        both = jnp.concatenate([odd[0].reshape(128, 256), odd[1].reshape(128, 256)], axis=0)
        lane = lax.rem(lax.broadcasted_iota(jnp.int32, (256, 256), 1), 64)
        real = jnp.where(lane < 32, both, 0.0).astype(BF)
        imag = jnp.where(lane < 32, 0.0, both).astype(BF)
        stacked = jnp.concatenate([real, imag], axis=0)
        traces = jnp.dot(first[...], stacked, preferred_element_type=F32).reshape(64, 8, 256)
        times = lax.broadcasted_iota(jnp.int32, (64, 8, 256), 0)
        kept[h] = jnp.where(times < onw[h][None], traces, 0.0).astype(BF).reshape(512, 256)

    def window_out(h):
        back = jnp.dot(second[...], kept[h], preferred_element_type=F32)
        lane = lax.rem(lax.broadcasted_iota(jnp.int32, (64, 256), 1), 64)
        chosen = jnp.where(lane < 32, back[:64], back[64:]).reshape(2, 4, 8, 256)
        return jnp.concatenate(
            [jnp.concatenate([chosen[0, :, :, 64 * a:64 * a + 64], chosen[1, :, :, 64 * a:64 * a + 64]], axis=2)
             for a in range(4)], axis=1)

    def unpack(source, out):
        for q in range(Q):
            for i in range(R4):
                for o in range(2):
                    out[q * F + 2 * i + o] = jnp.concatenate(
                        [source[h * Q + q, i][:, 64 * o + 32 * e:64 * o + 32 * e + 32] for e in range(2) for h in range(CHAINS)],
                        axis=1)

    def total(r, it, q, keep):
        def step(f, carry):
            acc = r[it, q, 0, f].astype(F32)
            for i in range(1, 8):
                acc = acc + r[it, q, i, f].astype(F32)
            keep[it, q, fme, f] = acc.astype(BF)
            return carry
        lax.fori_loop(0, R4, step, 0, unroll=True)

    low = lax.broadcasted_iota(jnp.int32, (256, 128), 1) < 64

    def iteration(it, carry):
        for s in range(S):
            pblk[it, s, own] = plus[it, s]
        for s in range(S):
            q = s % Q
            all_plus(it, s).wait_recv()

            if s < Q:
                @pl.when(it == 0)
                def _():
                    all_reflection(q).wait_recv()

            def forward(i, carry):
                block = pblk[it, s, :, i].reshape(256, 128)
                other = turned(block, 1)
                out = [jnp.dot(rblk[q, :, 2 * i + o, 0].reshape(256, 256), block, preferred_element_type=F32)
                       + jnp.dot(rblk[q, :, 2 * i + o, 1].reshape(256, 256), other, preferred_element_type=F32)
                       for o in range(2)]
                s1[it, s, :, i] = jnp.where(low, out[0], out[1]).astype(BF).reshape(8, 32, 128)
                return carry
            lax.fori_loop(0, R4, forward, 0, unroll=True)
            for d, cp in ring:
                send_rows(it, s, d, cp).start()
            partner_rows(it, s).start()
            r1[it, s, c] = s1[it, s, mine]

        @pl.when(it == 0)
        def _():
            for q in range(Q):
                def flip(i, carry):
                    for part in range(2):
                        rtrans[q * F + i, part] = rblk[q, :, i, part].reshape(256, 256).T
                    return carry
                lax.fori_loop(0, F, flip, 0)

        for s in range(S):
            all_rows(it, s).wait_recv()
            total(r1, it, s, xf1)
            for d in (2, 1, 3):
                send_freq(xf1, it, s, d, 2).start()

        for h in range(CHAINS):
            for s in range(h * Q, h * Q + Q):
                all_freq(xf1, it, s, 2).wait_recv()
            window_in(xf1, it, h)
            value = window_out(h).astype(BF)
            for q in range(Q):
                s = h * Q + q
                minus[it, s] = value[q * R4:(q + 1) * R4]
                for d, cp in ring:
                    send_minus(it, s, d, cp).start()
                partner_minus(it, s).start()
                mblk[it, s, mine] = minus[it, s]
        for s in range(S):
            q = s % Q
            all_minus(it, s).wait_recv()

            def adjoint(i, carry):
                block = mblk[it, s, :, i].reshape(256, 128)
                other = turned(block, -1)
                out = [jnp.dot(rtrans[q * F + 2 * i + o, 0], block, preferred_element_type=F32)
                       + jnp.dot(rtrans[q * F + 2 * i + o, 1], other, preferred_element_type=F32)
                       for o in range(2)]
                s2[it, s, :, i] = jnp.where(low, out[0], out[1]).astype(BF).reshape(8, 32, 128)
                return carry
            lax.fori_loop(0, R4, adjoint, 0, unroll=True)
            for du, dz in around:
                send_sources(it, s, du, dz).start()
            r2[it, s, 0] = s2[it, s, own]
        for s in range(S):
            all_sources(it, s).wait_recv()
            total(r2, it, s, xf2)
            for d in (2, 1, 3):
                send_freq(xf2, it, s, d, 5).start()
        for h in range(CHAINS):
            for s in range(h * Q, h * Q + Q):
                all_freq(xf2, it, s, 5).wait_recv()
            window_in(xf2, it, h)
            value = window_out(h)
            for q in range(Q):
                s = h * Q + q
                plus[it + 1, s] = (packed[s].astype(F32) + value[q * R4:(q + 1) * R4]).astype(BF)

                @pl.when(it + 1 < ITERS)
                def _():
                    for du, dz in around:
                        send_plus(it + 1, s, du, dz).start()

        for s in range(S):
            for copies in (all_plus(it, s), all_rows(it, s), all_freq(xf1, it, s, 2), all_minus(it, s),
                           all_sources(it, s), all_freq(xf2, it, s, 5)):
                copies.wait_send()
        return carry

    lax.fori_loop(0, ITERS, iteration, 0)
    unpack(minus.at[ITERS - 1], minus_out)
    unpack(plus.at[ITERS], plus_out)
    for q in range(Q):
        all_reflection(q).wait_send()


def local(reflection, focus_direct, onsets):
    first, second = window_tables()
    block = jax.ShapeDtypeStruct((8, 32, 128), BF)
    vmem = pl.BlockSpec(memory_space=pltpu.VMEM)
    part = (R4, 32, 128)
    return pl.pallas_call(
        kernel,
        out_shape=(block, block),
        in_specs=[pl.BlockSpec(memory_space=pltpu.HBM)] * 5,
        out_specs=(vmem, vmem),
        scratch_shapes=[
            pltpu.VMEM((8, 2, 32, 2048), BF),
            pltpu.VMEM((8, 32, 128), BF),
            pltpu.VMEM((32, 64), jnp.int32),
            pltpu.VMEM((512, 512), BF),
            pltpu.VMEM((128, 512), BF),
            pltpu.VMEM((Q, 8, F, 2, 32, 256), BF),
            pltpu.VMEM((Q, 8, F, 2, 32, 256), BF),
            pltpu.VMEM((8, 2, 256, 256), BF),
            pltpu.VMEM((ITERS + 1, S) + part, BF),
            pltpu.VMEM((ITERS, S, 8) + part, BF),
            pltpu.VMEM((ITERS, S, 8) + part, BF),
            pltpu.VMEM((ITERS, S, 8) + part, BF),
            pltpu.VMEM((ITERS, S, 4) + part, BF),
            pltpu.VMEM((ITERS, S) + part, BF),
            pltpu.VMEM((ITERS, S, 8) + part, BF),
            pltpu.VMEM((ITERS, S, 8) + part, BF),
            pltpu.VMEM((ITERS, S, 8) + part, BF),
            pltpu.VMEM((ITERS, S, 4) + part, BF),
            pltpu.VMEM((2, 512, 256), BF),
            pltpu.VMEM((2, 8, 256), jnp.int32),
            pltpu.VMEM((S,) + part, BF),
            pltpu.SemaphoreType.DMA((5,)),
            pltpu.SemaphoreType.DMA((Q,)),
            pltpu.SemaphoreType.DMA((Q,)),
            pltpu.SemaphoreType.DMA((ITERS, S, 6)),
            pltpu.SemaphoreType.DMA((ITERS, S, 6)),
        ],
        compiler_params=pltpu.CompilerParams(
            collective_id=0, has_side_effects=True, vmem_limit_bytes=40 * 1024 * 1024),
        name="marchenko",
    )(*[pltpu.with_memory_space_constraint(a, pltpu.HBM)
        for a in (reflection, focus_direct, onsets, jnp.asarray(first), jnp.asarray(second))])


def solution(mesh):
    in_specs = (P("freq", None, "rows", None), P("freq", "rows", None), P("rows", None))
    out_specs = (P("freq", "rows", None), P("freq", "rows", None))
    return jax.shard_map(local, mesh=mesh, in_specs=in_specs, out_specs=out_specs, check_vma=False)
```

```python
import math

import jax
import jax.numpy as jnp
import numpy as np
from jax import lax
from jax.experimental import pallas as pl
from jax.experimental.pallas import tpu as pltpu
from jax.sharding import PartitionSpec as P

NT = 128
ITERS = 2
MESH = pl.DeviceIdType.MESH
BF = jnp.bfloat16
F32 = jnp.float32
Q = 2
CHAINS = 2
S = CHAINS * Q
R4 = 4 // Q
F = 8 // Q


def window_tables():
    t = np.arange(64)[:, None]
    k = np.arange(1, 33)[None, :]
    ang = 2.0 * np.pi * ((t * k) % NT) / NT
    parts = np.stack([np.cos(ang), np.sin(ang)])
    eye = np.eye(8)
    paired = parts.reshape(2, 64, 4, Q, R4, 2)
    first = np.einsum("ctgqfo,rs->trcoqgfs", paired, eye).reshape(512, 512)
    weight = np.where(np.arange(64) == 0, 2.0, 4.0) / NT
    back = paired * weight[None, :, None, None, None, None]
    second = np.einsum("ctgqfo,rs->gcoqfrts", back, eye).reshape(4, 128, 512)
    return first.astype(jnp.bfloat16), second.astype(jnp.bfloat16)


def turned(block, sign):
    p = [block[:, 32 * i:32 * i + 32] for i in range(4)]
    if sign > 0:
        return jnp.concatenate([-p[1], p[0], -p[3], p[2]], axis=1)
    return jnp.concatenate([p[1], -p[0], p[3], -p[2]], axis=1)


def kernel(refl_hbm, direct_hbm, onsets_hbm, first_hbm, second_hbm, plus_out, minus_out,
           refl, direct, onsets, first, second,
           rsend, rblk, rtrans, plus, pblk, s1, r1, xf1, minus, mblk, s2, r2, xf2, kept, onw, packed,
           lsem, rsnd, rrcv, ssem, rsem):
    fme = lax.axis_index("freq")
    row = lax.axis_index("rows")
    c = lax.rem(row, 2)
    x = lax.rem(row // 2, 4)
    z = lax.rem(row // 8, 2)
    y = row // 16
    zero = c == 0
    u = jnp.where(zero, y, x)
    v = jnp.where(zero, x, y)

    def rows(y, z, x, c):
        return ((y * 2 + z) * 4 + x) * 2 + c

    def wrap(a):
        return lax.rem(a + 8, 4)

    def ring_u(du, dz):
        up, zp = wrap(u + du), lax.rem(z + dz, 2)
        return (fme, jnp.where(zero, rows(up, zp, x, c), rows(y, zp, up, c)))

    def to_ring(d, cp):
        return (fme, rows(y, z, wrap(x + d), 0) if cp == 0 else rows(wrap(y + d), z, x, 1))

    def on_ring(d, cp):
        vp = wrap(v + d)
        return (fme, jnp.where(zero, rows(y, z, vp, cp), rows(vp, z, x, cp)))

    partner = (fme, rows(y, z, x, 1 - c))

    def freq_on(d):
        return (wrap(fme + d), row)

    around = [(du, dz) for dz in (1, 0) for du in (2, 1, 3, 0) if (du, dz) != (0, 0)]
    ring = [(d, cp) for d in (2, 1, 3) for cp in range(2)]

    bar = pltpu.get_barrier_semaphore()
    peers = [partner]
    peers += [ring_u(du, dz) for du, dz in around]
    peers += [to_ring(d, cp) for d, cp in ring]
    peers += [on_ring(d, cp) for d, cp in ring]
    peers += [freq_on(d) for d in range(1, 4)]
    for q in peers:
        pl.semaphore_signal(bar, inc=1, device_id=q, device_id_type=MESH)
    loads = [pltpu.make_async_copy(refl_hbm, refl, lsem.at[0]), pltpu.make_async_copy(direct_hbm, direct, lsem.at[1]),
             pltpu.make_async_copy(onsets_hbm, onsets, lsem.at[2]), pltpu.make_async_copy(first_hbm, first, lsem.at[3]),
             pltpu.make_async_copy(second_hbm.at[fme], second, lsem.at[4])]
    for load in loads:
        load.start()

    def copy(src, dst, send, recv, device):
        return pltpu.make_async_remote_copy(
            src_ref=src, dst_ref=dst, send_sem=send, recv_sem=recv, device_id=device, device_id_type=MESH)

    def pieces(cp, w):
        if cp == 0:
            return [(k * 256 + w * 64) for k in range(8)]
        return [((w * 2 + k % 2) * 256 + (k // 2) * 64 + 32) for k in range(8)]

    def arrange(q):
        def step(i, carry):
            block = refl[q * F + i].reshape(64, 2048)
            for cp in range(2):
                for w in range(4):
                    out = jnp.concatenate([block[:, p:p + 32] for p in pieces(cp, w)], axis=1)
                    rsend[q, cp * 4 + w, i] = out.reshape(2, 32, 256)
            return carry
        lax.fori_loop(0, F, step, 0)

    mine = v * 2 + c
    own = u * 2 + z

    def send_reflection(q, d, cp):
        place = x if cp == 0 else y
        return copy(rsend.at[q, cp * 4 + wrap(place + d)], rblk.at[q, place * 2 + c],
                    rsnd.at[q], rrcv.at[q], to_ring(d, cp))

    def partner_reflection(q):
        return copy(rsend.at[q, (1 - c) * 4 + u], rblk.at[q, u * 2 + c], rsnd.at[q], rrcv.at[q], partner)

    def wait_for(buffer, count, send, recv):
        return copy(buffer.at[pl.ds(0, count)], buffer.at[pl.ds(0, count)], send, recv, partner)

    def all_reflection(q):
        return wait_for(rblk.at[q], 7, rsnd.at[q], rrcv.at[q])

    def stage(it, q, n):
        return ssem.at[it, q, n], rsem.at[it, q, n]

    def send_plus(it, q, du, dz):
        return copy(plus.at[it, q], pblk.at[it, q, own], *stage(it, q, 0), ring_u(du, dz))

    def all_plus(it, q):
        return wait_for(pblk.at[it, q], 7, *stage(it, q, 0))

    def send_rows(it, q, d, cp):
        return copy(s1.at[it, q, wrap(v + d) * 2 + cp], r1.at[it, q, d * 2 + c], *stage(it, q, 1), on_ring(d, cp))

    def partner_rows(it, q):
        return copy(s1.at[it, q, v * 2 + 1 - c], r1.at[it, q, c], *stage(it, q, 1), partner)

    def all_rows(it, q):
        return wait_for(r1.at[it, q], 7, *stage(it, q, 1))

    def send_freq(xf, it, q, d, n):
        return copy(xf.at[it, q, fme], xf.at[it, q, fme], *stage(it, q, n), freq_on(d))

    def all_freq(xf, it, q, n):
        return wait_for(xf.at[it, q], 3, *stage(it, q, n))

    def send_minus(it, q, d, cp):
        place = x if cp == 0 else y
        return copy(minus.at[it, q], mblk.at[it, q, place * 2 + c], *stage(it, q, 3), to_ring(d, cp))

    def partner_minus(it, q):
        return copy(minus.at[it, q], mblk.at[it, q, u * 2 + c], *stage(it, q, 3), partner)

    def all_minus(it, q):
        return wait_for(mblk.at[it, q], 7, *stage(it, q, 3))

    def send_sources(it, q, du, dz):
        i = du * 2 + dz
        return copy(s2.at[it, q, wrap(u + du) * 2 + lax.rem(z + dz, 2)], r2.at[it, q, i], *stage(it, q, 4), ring_u(du, dz))

    def all_sources(it, q):
        return wait_for(r2.at[it, q], 7, *stage(it, q, 4))

    loads[1].wait()
    for s in range(S):
        h, q = s // Q, s % Q
        for i in range(R4):
            pair = [direct[q * F + 2 * i + o] for o in range(2)]
            value = jnp.concatenate([pair[o][:, e:e + 32] for o in range(2) for e in (32 * h, 64 + 32 * h)], axis=1)
            packed[s, i] = value
            plus[0, s, i] = value
    loads[0].wait()
    for q in range(Q):
        arrange(q)
        if q == 0:
            pl.semaphore_wait(bar, len(peers))
        for d, cp in ring:
            send_reflection(q, d, cp).start()
        partner_reflection(q).start()
        for h in range(CHAINS):
            for du, dz in around:
                send_plus(0, h * Q + q, du, dz).start()
        rblk[q, mine] = rsend[q, c * 4 + v]

    loads[2].wait()
    on = onsets[...]
    for h in range(CHAINS):
        eight = [on[8 * a:8 * a + 8, 32 * h:32 * h + 32] for a in range(4)]
        onw[h] = jnp.concatenate([eight[a] for a in range(4) for _ in range(2)], axis=1)
    loads[3].wait()
    loads[4].wait()

    def window_in(xf, it, h):
        spec = jnp.concatenate([xf[it, h * Q + q].reshape(4 * R4, 32, 128) for q in range(Q)], axis=0).astype(F32)
        odd = [jnp.concatenate([spec[:, 8 * a:8 * a + 8, 64 * o:64 * o + 64] for a in range(4)], axis=2) for o in range(2)]
        both = jnp.concatenate([odd[0].reshape(128, 256), odd[1].reshape(128, 256)], axis=0)
        lane = lax.rem(lax.broadcasted_iota(jnp.int32, (256, 256), 1), 64)
        real = jnp.where(lane < 32, both, 0.0).astype(BF)
        imag = jnp.where(lane < 32, 0.0, both).astype(BF)
        stacked = jnp.concatenate([real, imag], axis=0)
        traces = jnp.dot(first[...], stacked, preferred_element_type=F32).reshape(64, 8, 256)
        times = lax.broadcasted_iota(jnp.int32, (64, 8, 256), 0)
        kept[h] = jnp.where(times < onw[h][None], traces, 0.0).astype(BF).reshape(512, 256)

    def window_out(h):
        back = jnp.dot(second[...], kept[h], preferred_element_type=F32)
        lane = lax.rem(lax.broadcasted_iota(jnp.int32, (64, 256), 1), 64)
        chosen = jnp.where(lane < 32, back[:64], back[64:]).reshape(2, 4, 8, 256)
        return jnp.concatenate(
            [jnp.concatenate([chosen[0, :, :, 64 * a:64 * a + 64], chosen[1, :, :, 64 * a:64 * a + 64]], axis=2)
             for a in range(4)], axis=1)

    def unpack(source, out):
        for q in range(Q):
            for i in range(R4):
                for o in range(2):
                    out[q * F + 2 * i + o] = jnp.concatenate(
                        [source[h * Q + q, i][:, 64 * o + 32 * e:64 * o + 32 * e + 32] for e in range(2) for h in range(CHAINS)],
                        axis=1)

    def total(r, it, q, keep):
        def step(f, carry):
            acc = r[it, q, 0, f].astype(F32)
            for i in range(1, 8):
                acc = acc + r[it, q, i, f].astype(F32)
            keep[it, q, fme, f] = acc.astype(BF)
            return carry
        lax.fori_loop(0, R4, step, 0, unroll=True)

    low = lax.broadcasted_iota(jnp.int32, (256, 128), 1) < 64

    def iteration(it, carry):
        for s in range(S):
            pblk[it, s, own] = plus[it, s]
        for s in range(S):
            q = s % Q
            all_plus(it, s).wait_recv()

            if s < Q:
                @pl.when(it == 0)
                def _():
                    all_reflection(q).wait_recv()

            def forward(i, carry):
                block = pblk[it, s, :, i].reshape(256, 128)
                other = turned(block, 1)
                out = [jnp.dot(rblk[q, :, 2 * i + o, 0].reshape(256, 256), block, preferred_element_type=F32)
                       + jnp.dot(rblk[q, :, 2 * i + o, 1].reshape(256, 256), other, preferred_element_type=F32)
                       for o in range(2)]
                s1[it, s, :, i] = jnp.where(low, out[0], out[1]).astype(BF).reshape(8, 32, 128)
                return carry
            lax.fori_loop(0, R4, forward, 0, unroll=True)
            for d, cp in ring:
                send_rows(it, s, d, cp).start()
            partner_rows(it, s).start()
            r1[it, s, c] = s1[it, s, mine]

        @pl.when(it == 0)
        def _():
            for q in range(Q):
                def flip(i, carry):
                    for part in range(2):
                        rtrans[q * F + i, part] = rblk[q, :, i, part].reshape(256, 256).T
                    return carry
                lax.fori_loop(0, F, flip, 0)

        for s in range(S):
            all_rows(it, s).wait_recv()
            total(r1, it, s, xf1)
            for d in (2, 1, 3):
                send_freq(xf1, it, s, d, 2).start()

        for h in range(CHAINS):
            for s in range(h * Q, h * Q + Q):
                all_freq(xf1, it, s, 2).wait_recv()
            window_in(xf1, it, h)
            value = window_out(h).astype(BF)
            for q in range(Q):
                s = h * Q + q
                minus[it, s] = value[q * R4:(q + 1) * R4]
                for d, cp in ring:
                    send_minus(it, s, d, cp).start()
                partner_minus(it, s).start()
                mblk[it, s, mine] = minus[it, s]
        for s in range(S):
            q = s % Q
            all_minus(it, s).wait_recv()

            def adjoint(i, carry):
                block = mblk[it, s, :, i].reshape(256, 128)
                other = turned(block, -1)
                out = [jnp.dot(rtrans[q * F + 2 * i + o, 0], block, preferred_element_type=F32)
                       + jnp.dot(rtrans[q * F + 2 * i + o, 1], other, preferred_element_type=F32)
                       for o in range(2)]
                s2[it, s, :, i] = jnp.where(low, out[0], out[1]).astype(BF).reshape(8, 32, 128)
                return carry
            lax.fori_loop(0, R4, adjoint, 0, unroll=True)
            for du, dz in around:
                send_sources(it, s, du, dz).start()
            r2[it, s, 0] = s2[it, s, own]
        for s in range(S):
            all_sources(it, s).wait_recv()
            total(r2, it, s, xf2)
            for d in (2, 1, 3):
                send_freq(xf2, it, s, d, 5).start()

        @pl.when(it + 1 == ITERS)
        def _():
            unpack(minus.at[it], minus_out)

        for h in range(CHAINS):
            for s in range(h * Q, h * Q + Q):
                all_freq(xf2, it, s, 5).wait_recv()
            window_in(xf2, it, h)
            value = window_out(h)
            for q in range(Q):
                s = h * Q + q
                plus[it + 1, s] = (packed[s].astype(F32) + value[q * R4:(q + 1) * R4]).astype(BF)

                @pl.when(it + 1 < ITERS)
                def _():
                    for du, dz in around:
                        send_plus(it + 1, s, du, dz).start()

        for s in range(S):
            for copies in (all_plus(it, s), all_rows(it, s), all_freq(xf1, it, s, 2), all_minus(it, s),
                           all_sources(it, s), all_freq(xf2, it, s, 5)):
                copies.wait_send()
        return carry

    lax.fori_loop(0, ITERS, iteration, 0)
    unpack(plus.at[ITERS], plus_out)
    for q in range(Q):
        all_reflection(q).wait_send()


def local(reflection, focus_direct, onsets):
    first, second = window_tables()
    block = jax.ShapeDtypeStruct((8, 32, 128), BF)
    vmem = pl.BlockSpec(memory_space=pltpu.VMEM)
    part = (R4, 32, 128)
    return pl.pallas_call(
        kernel,
        out_shape=(block, block),
        in_specs=[pl.BlockSpec(memory_space=pltpu.HBM)] * 5,
        out_specs=(vmem, vmem),
        scratch_shapes=[
            pltpu.VMEM((8, 2, 32, 2048), BF),
            pltpu.VMEM((8, 32, 128), BF),
            pltpu.VMEM((32, 64), jnp.int32),
            pltpu.VMEM((512, 512), BF),
            pltpu.VMEM((128, 512), BF),
            pltpu.VMEM((Q, 8, F, 2, 32, 256), BF),
            pltpu.VMEM((Q, 8, F, 2, 32, 256), BF),
            pltpu.VMEM((8, 2, 256, 256), BF),
            pltpu.VMEM((ITERS + 1, S) + part, BF),
            pltpu.VMEM((ITERS, S, 8) + part, BF),
            pltpu.VMEM((ITERS, S, 8) + part, BF),
            pltpu.VMEM((ITERS, S, 8) + part, BF),
            pltpu.VMEM((ITERS, S, 4) + part, BF),
            pltpu.VMEM((ITERS, S) + part, BF),
            pltpu.VMEM((ITERS, S, 8) + part, BF),
            pltpu.VMEM((ITERS, S, 8) + part, BF),
            pltpu.VMEM((ITERS, S, 8) + part, BF),
            pltpu.VMEM((ITERS, S, 4) + part, BF),
            pltpu.VMEM((2, 512, 256), BF),
            pltpu.VMEM((2, 8, 256), jnp.int32),
            pltpu.VMEM((S,) + part, BF),
            pltpu.SemaphoreType.DMA((5,)),
            pltpu.SemaphoreType.DMA((Q,)),
            pltpu.SemaphoreType.DMA((Q,)),
            pltpu.SemaphoreType.DMA((ITERS, S, 6)),
            pltpu.SemaphoreType.DMA((ITERS, S, 6)),
        ],
        compiler_params=pltpu.CompilerParams(
            collective_id=0, has_side_effects=True, vmem_limit_bytes=40 * 1024 * 1024),
        name="marchenko",
    )(*[pltpu.with_memory_space_constraint(a, pltpu.HBM)
        for a in (reflection, focus_direct, onsets, jnp.asarray(first), jnp.asarray(second))])


def solution(mesh):
    in_specs = (P("freq", None, "rows", None), P("freq", "rows", None), P("rows", None))
    out_specs = (P("freq", "rows", None), P("freq", "rows", None))
    return jax.shard_map(local, mesh=mesh, in_specs=in_specs, out_specs=out_specs, check_vma=False)
```

```python
import math

import jax
import jax.numpy as jnp
import numpy as np
from jax import lax
from jax.experimental import pallas as pl
from jax.experimental.pallas import tpu as pltpu
from jax.sharding import PartitionSpec as P

NT = 128
ITERS = 2
MESH = pl.DeviceIdType.MESH
BF = jnp.bfloat16
F32 = jnp.float32
Q = 2
CHAINS = 2
S = CHAINS * Q
R4 = 4 // Q
F = 8 // Q


def window_tables():
    t = np.arange(64)[:, None]
    k = np.arange(1, 33)[None, :]
    ang = 2.0 * np.pi * ((t * k) % NT) / NT
    parts = np.stack([np.cos(ang), np.sin(ang)])
    eye = np.eye(8)
    paired = parts.reshape(2, 64, 4, Q, R4, 2)
    first = np.einsum("ctgqfo,rs->trcoqgfs", paired, eye).reshape(512, 512)
    weight = np.where(np.arange(64) == 0, 2.0, 4.0) / NT
    back = paired * weight[None, :, None, None, None, None]
    second = np.einsum("ctgqfo,rs->gcoqfrts", back, eye).reshape(4, 128, 512)
    return first.astype(jnp.bfloat16), second.astype(jnp.bfloat16)


def turned(block, sign):
    p = [block[:, 32 * i:32 * i + 32] for i in range(4)]
    if sign > 0:
        return jnp.concatenate([-p[1], p[0], -p[3], p[2]], axis=1)
    return jnp.concatenate([p[1], -p[0], p[3], -p[2]], axis=1)


def kernel(refl_hbm, direct_hbm, onsets_hbm, first_hbm, second_hbm, plus_out, minus_out,
           refl, direct, onsets, first, second,
           rsend, rblk, rtrans, plus, pblk, s1, r1, xf1, minus, mblk, s2, r2, xf2, kept, onw, packed,
           lsem, rsnd, rrcv, ssem, rsem):
    fme = lax.axis_index("freq")
    row = lax.axis_index("rows")
    c = lax.rem(row, 2)
    x = lax.rem(row // 2, 4)
    z = lax.rem(row // 8, 2)
    y = row // 16
    zero = c == 0
    u = jnp.where(zero, y, x)
    v = jnp.where(zero, x, y)

    def rows(y, z, x, c):
        return ((y * 2 + z) * 4 + x) * 2 + c

    def wrap(a):
        return lax.rem(a + 8, 4)

    def ring_u(du, dz):
        up, zp = wrap(u + du), lax.rem(z + dz, 2)
        return (fme, jnp.where(zero, rows(up, zp, x, c), rows(y, zp, up, c)))

    def to_ring(d, cp):
        return (fme, rows(y, z, wrap(x + d), 0) if cp == 0 else rows(wrap(y + d), z, x, 1))

    def on_ring(d, cp):
        vp = wrap(v + d)
        return (fme, jnp.where(zero, rows(y, z, vp, cp), rows(vp, z, x, cp)))

    partner = (fme, rows(y, z, x, 1 - c))

    def freq_on(d):
        return (wrap(fme + d), row)

    around = [(du, dz) for dz in (1, 0) for du in (2, 1, 3, 0) if (du, dz) != (0, 0)]
    ring = [(d, cp) for d in (2, 1, 3) for cp in range(2)]

    bar = pltpu.get_barrier_semaphore()
    peers = [partner]
    peers += [ring_u(du, dz) for du, dz in around]
    peers += [to_ring(d, cp) for d, cp in ring]
    peers += [on_ring(d, cp) for d, cp in ring]
    peers += [freq_on(d) for d in range(1, 4)]
    for q in peers:
        pl.semaphore_signal(bar, inc=1, device_id=q, device_id_type=MESH)
    loads = [pltpu.make_async_copy(refl_hbm, refl, lsem.at[0]), pltpu.make_async_copy(direct_hbm, direct, lsem.at[1]),
             pltpu.make_async_copy(onsets_hbm, onsets, lsem.at[2]), pltpu.make_async_copy(first_hbm, first, lsem.at[3]),
             pltpu.make_async_copy(second_hbm.at[fme], second, lsem.at[4])]
    for load in loads:
        load.start()

    def copy(src, dst, send, recv, device):
        return pltpu.make_async_remote_copy(
            src_ref=src, dst_ref=dst, send_sem=send, recv_sem=recv, device_id=device, device_id_type=MESH)

    def pieces(cp, w):
        if cp == 0:
            return [(k * 256 + w * 64) for k in range(8)]
        return [((w * 2 + k % 2) * 256 + (k // 2) * 64 + 32) for k in range(8)]

    def arrange(q):
        def step(i, carry):
            block = refl[q * F + i].reshape(64, 2048)
            for cp in range(2):
                for w in range(4):
                    out = jnp.concatenate([block[:, p:p + 32] for p in pieces(cp, w)], axis=1)
                    rsend[q, cp * 4 + w, i] = out.reshape(2, 32, 256)
            return carry
        lax.fori_loop(0, F, step, 0)

    mine = v * 2 + c
    own = u * 2 + z

    def send_reflection(q, d, cp):
        place = x if cp == 0 else y
        return copy(rsend.at[q, cp * 4 + wrap(place + d)], rblk.at[q, place * 2 + c],
                    rsnd.at[q], rrcv.at[q], to_ring(d, cp))

    def partner_reflection(q):
        return copy(rsend.at[q, (1 - c) * 4 + u], rblk.at[q, u * 2 + c], rsnd.at[q], rrcv.at[q], partner)

    def wait_for(buffer, count, send, recv):
        return copy(buffer.at[pl.ds(0, count)], buffer.at[pl.ds(0, count)], send, recv, partner)

    def all_reflection(q):
        return wait_for(rblk.at[q], 7, rsnd.at[q], rrcv.at[q])

    def stage(it, q, n):
        return ssem.at[it, q, n], rsem.at[it, q, n]

    def send_plus(it, q, du, dz):
        return copy(plus.at[it, q], pblk.at[it, q, own], *stage(it, q, 0), ring_u(du, dz))

    def all_plus(it, q):
        return wait_for(pblk.at[it, q], 7, *stage(it, q, 0))

    def send_rows(it, q, d, cp):
        return copy(s1.at[it, q, wrap(v + d) * 2 + cp], r1.at[it, q, d * 2 + c], *stage(it, q, 1), on_ring(d, cp))

    def partner_rows(it, q):
        return copy(s1.at[it, q, v * 2 + 1 - c], r1.at[it, q, c], *stage(it, q, 1), partner)

    def all_rows(it, q):
        return wait_for(r1.at[it, q], 7, *stage(it, q, 1))

    def send_freq(xf, it, q, d, n):
        return copy(xf.at[it, q, fme], xf.at[it, q, fme], *stage(it, q, n), freq_on(d))

    def all_freq(xf, it, q, n):
        return wait_for(xf.at[it, q], 3, *stage(it, q, n))

    def send_minus(it, q, d, cp):
        place = x if cp == 0 else y
        return copy(minus.at[it, q], mblk.at[it, q, place * 2 + c], *stage(it, q, 3), to_ring(d, cp))

    def partner_minus(it, q):
        return copy(minus.at[it, q], mblk.at[it, q, u * 2 + c], *stage(it, q, 3), partner)

    def all_minus(it, q):
        return wait_for(mblk.at[it, q], 7, *stage(it, q, 3))

    def send_sources(it, q, du, dz):
        i = du * 2 + dz
        return copy(s2.at[it, q, wrap(u + du) * 2 + lax.rem(z + dz, 2)], r2.at[it, q, i], *stage(it, q, 4), ring_u(du, dz))

    def all_sources(it, q):
        return wait_for(r2.at[it, q], 7, *stage(it, q, 4))

    loads[1].wait()
    for s in range(S):
        h, q = s // Q, s % Q
        for i in range(R4):
            pair = [direct[q * F + 2 * i + o] for o in range(2)]
            value = jnp.concatenate([pair[o][:, e:e + 32] for o in range(2) for e in (32 * h, 64 + 32 * h)], axis=1)
            packed[s, i] = value
            plus[0, s, i] = value
    loads[0].wait()
    for q in range(Q):
        arrange(q)
        if q == 0:
            pl.semaphore_wait(bar, len(peers))
        for d, cp in ring:
            send_reflection(q, d, cp).start()
        partner_reflection(q).start()
        for h in range(CHAINS):
            for du, dz in around:
                send_plus(0, h * Q + q, du, dz).start()
        rblk[q, mine] = rsend[q, c * 4 + v]

    loads[2].wait()
    on = onsets[...]
    for h in range(CHAINS):
        eight = [on[8 * a:8 * a + 8, 32 * h:32 * h + 32] for a in range(4)]
        onw[h] = jnp.concatenate([eight[a] for a in range(4) for _ in range(2)], axis=1)
    loads[3].wait()
    loads[4].wait()

    def window_in(xf, it, h):
        spec = jnp.concatenate([xf[it, h * Q + q].reshape(4 * R4, 32, 128) for q in range(Q)], axis=0).astype(F32)
        odd = [jnp.concatenate([spec[:, 8 * a:8 * a + 8, 64 * o:64 * o + 64] for a in range(4)], axis=2) for o in range(2)]
        both = jnp.concatenate([odd[0].reshape(128, 256), odd[1].reshape(128, 256)], axis=0)
        lane = lax.rem(lax.broadcasted_iota(jnp.int32, (256, 256), 1), 64)
        real = jnp.where(lane < 32, both, 0.0).astype(BF)
        imag = jnp.where(lane < 32, 0.0, both).astype(BF)
        stacked = jnp.concatenate([real, imag], axis=0)
        traces = jnp.dot(first[...], stacked, preferred_element_type=F32).reshape(64, 8, 256)
        times = lax.broadcasted_iota(jnp.int32, (64, 8, 256), 0)
        kept[h] = jnp.where(times < onw[h][None], traces, 0.0).astype(BF).reshape(512, 256)

    def window_out(h):
        back = jnp.dot(second[...], kept[h], preferred_element_type=F32)
        lane = lax.rem(lax.broadcasted_iota(jnp.int32, (64, 256), 1), 64)
        chosen = jnp.where(lane < 32, back[:64], back[64:]).reshape(2, 4, 8, 256)
        return jnp.concatenate(
            [jnp.concatenate([chosen[0, :, :, 64 * a:64 * a + 64], chosen[1, :, :, 64 * a:64 * a + 64]], axis=2)
             for a in range(4)], axis=1)

    def unpack(source, out):
        for q in range(Q):
            for i in range(R4):
                for o in range(2):
                    out[q * F + 2 * i + o] = jnp.concatenate(
                        [source[h * Q + q, i][:, 64 * o + 32 * e:64 * o + 32 * e + 32] for e in range(2) for h in range(CHAINS)],
                        axis=1)

    def total(r, it, q, keep):
        def step(f, carry):
            acc = r[it, q, 0, f].astype(F32)
            for i in range(1, 8):
                acc = acc + r[it, q, i, f].astype(F32)
            keep[it, q, fme, f] = acc.astype(BF)
            return carry
        lax.fori_loop(0, R4, step, 0, unroll=True)

    low = lax.broadcasted_iota(jnp.int32, (256, 128), 1) < 64

    def iteration(it, carry):
        for s in range(S):
            pblk[it, s, own] = plus[it, s]
        for s in range(S):
            q = s % Q
            all_plus(it, s).wait_recv()

            if s < Q:
                @pl.when(it == 0)
                def _():
                    all_reflection(q).wait_recv()

            def forward(i, carry):
                block = pblk[it, s, :, i].reshape(256, 128)
                other = turned(block, 1)
                out = [jnp.dot(rblk[q, :, 2 * i + o, 0].reshape(256, 256), block, preferred_element_type=F32)
                       + jnp.dot(rblk[q, :, 2 * i + o, 1].reshape(256, 256), other, preferred_element_type=F32)
                       for o in range(2)]
                s1[it, s, :, i] = jnp.where(low, out[0], out[1]).astype(BF).reshape(8, 32, 128)
                return carry
            lax.fori_loop(0, R4, forward, 0, unroll=True)
            for d, cp in ring:
                send_rows(it, s, d, cp).start()
            partner_rows(it, s).start()
            r1[it, s, c] = s1[it, s, mine]

        @pl.when(it == 0)
        def _():
            for q in range(Q):
                def flip(i, carry):
                    for part in range(2):
                        rtrans[q * F + i, part] = rblk[q, :, i, part].reshape(256, 256).T
                    return carry
                lax.fori_loop(0, F, flip, 0)

        for s in range(S):
            all_rows(it, s).wait_recv()
            total(r1, it, s, xf1)
            for d in (2, 1, 3):
                send_freq(xf1, it, s, d, 2).start()

        for h in range(CHAINS):
            for s in range(h * Q, h * Q + Q):
                all_freq(xf1, it, s, 2).wait_recv()
            window_in(xf1, it, h)
            value = window_out(h).astype(BF)
            for q in range(Q):
                s = h * Q + q
                minus[it, s] = value[q * R4:(q + 1) * R4]
                for d, cp in ring:
                    send_minus(it, s, d, cp).start()
                partner_minus(it, s).start()
                mblk[it, s, mine] = minus[it, s]
        for s in range(S):
            q = s % Q
            all_minus(it, s).wait_recv()

            def adjoint(i, carry):
                block = mblk[it, s, :, i].reshape(256, 128)
                other = turned(block, -1)
                out = [jnp.dot(rtrans[q * F + 2 * i + o, 0], block, preferred_element_type=F32)
                       + jnp.dot(rtrans[q * F + 2 * i + o, 1], other, preferred_element_type=F32)
                       for o in range(2)]
                s2[it, s, :, i] = jnp.where(low, out[0], out[1]).astype(BF).reshape(8, 32, 128)
                return carry
            lax.fori_loop(0, R4, adjoint, 0, unroll=True)
            for du, dz in around:
                send_sources(it, s, du, dz).start()
            r2[it, s, 0] = s2[it, s, own]
        for s in range(S):
            all_sources(it, s).wait_recv()
            total(r2, it, s, xf2)
            for d in (2, 1, 3):
                send_freq(xf2, it, s, d, 5).start()

        @pl.when(it + 1 == ITERS)
        def _():
            unpack(minus.at[it], minus_out)

        for h in range(CHAINS):
            for s in range(h * Q, h * Q + Q):
                all_freq(xf2, it, s, 5).wait_recv()
            window_in(xf2, it, h)
            value = window_out(h)
            for q in range(Q):
                s = h * Q + q
                plus[it + 1, s] = (packed[s].astype(F32) + value[q * R4:(q + 1) * R4]).astype(BF)

                @pl.when(it + 1 < ITERS)
                def _():
                    for du, dz in around:
                        send_plus(it + 1, s, du, dz).start()

        return carry

    lax.fori_loop(0, ITERS, iteration, 0)
    unpack(plus.at[ITERS], plus_out)
    for it in range(ITERS):
        for s in range(S):
            for copies in (all_plus(it, s), all_rows(it, s), all_freq(xf1, it, s, 2), all_minus(it, s),
                           all_sources(it, s), all_freq(xf2, it, s, 5)):
                copies.wait_send()
    for q in range(Q):
        all_reflection(q).wait_send()


def local(reflection, focus_direct, onsets):
    first, second = window_tables()
    block = jax.ShapeDtypeStruct((8, 32, 128), BF)
    vmem = pl.BlockSpec(memory_space=pltpu.VMEM)
    part = (R4, 32, 128)
    return pl.pallas_call(
        kernel,
        out_shape=(block, block),
        in_specs=[pl.BlockSpec(memory_space=pltpu.HBM)] * 5,
        out_specs=(vmem, vmem),
        scratch_shapes=[
            pltpu.VMEM((8, 2, 32, 2048), BF),
            pltpu.VMEM((8, 32, 128), BF),
            pltpu.VMEM((32, 64), jnp.int32),
            pltpu.VMEM((512, 512), BF),
            pltpu.VMEM((128, 512), BF),
            pltpu.VMEM((Q, 8, F, 2, 32, 256), BF),
            pltpu.VMEM((Q, 8, F, 2, 32, 256), BF),
            pltpu.VMEM((8, 2, 256, 256), BF),
            pltpu.VMEM((ITERS + 1, S) + part, BF),
            pltpu.VMEM((ITERS, S, 8) + part, BF),
            pltpu.VMEM((ITERS, S, 8) + part, BF),
            pltpu.VMEM((ITERS, S, 8) + part, BF),
            pltpu.VMEM((ITERS, S, 4) + part, BF),
            pltpu.VMEM((ITERS, S) + part, BF),
            pltpu.VMEM((ITERS, S, 8) + part, BF),
            pltpu.VMEM((ITERS, S, 8) + part, BF),
            pltpu.VMEM((ITERS, S, 8) + part, BF),
            pltpu.VMEM((ITERS, S, 4) + part, BF),
            pltpu.VMEM((2, 512, 256), BF),
            pltpu.VMEM((2, 8, 256), jnp.int32),
            pltpu.VMEM((S,) + part, BF),
            pltpu.SemaphoreType.DMA((5,)),
            pltpu.SemaphoreType.DMA((Q,)),
            pltpu.SemaphoreType.DMA((Q,)),
            pltpu.SemaphoreType.DMA((ITERS, S, 6)),
            pltpu.SemaphoreType.DMA((ITERS, S, 6)),
        ],
        compiler_params=pltpu.CompilerParams(
            collective_id=0, has_side_effects=True, vmem_limit_bytes=40 * 1024 * 1024),
        name="marchenko",
    )(*[pltpu.with_memory_space_constraint(a, pltpu.HBM)
        for a in (reflection, focus_direct, onsets, jnp.asarray(first), jnp.asarray(second))])


def solution(mesh):
    in_specs = (P("freq", None, "rows", None), P("freq", "rows", None), P("rows", None))
    out_specs = (P("freq", "rows", None), P("freq", "rows", None))
    return jax.shard_map(local, mesh=mesh, in_specs=in_specs, out_specs=out_specs, check_vma=False)
```
